512 devices in a mesh: row: 64 (over x, z_hi, y), col: 8 (over z_lo, core).
Axes of the slice: x: 4, y: 4, z: 16 (z_hi: 4, z_lo: 4; z = z_hi * 4 + z_lo), core: 2. Of those that a mesh axis runs over, the one named last changes fastest.
Arguments:
- inputs: bfloat16 [512, 12288], P('row', 'col'), may hold values from -6 to 6
- cotangent: bfloat16 [512, 12288], P('row', 'col'), may hold values from -6 to 6
- w1_blocks: bfloat16 [4608, 128, 128], P(('row', 'col')), may hold values from -0.15625 to 0.15625
- w1_where: int32 [4608], P(('row', 'col')), may hold values from 0 to 36863, as said below
- w2_blocks: bfloat16 [4608, 128, 128], P(('row', 'col')), may hold values from -0.078125 to 0.078125
- w2_where: int32 [4608], P(('row', 'col')), may hold values from 0 to 36863, as said below
Outputs:
- input_grad: bfloat16 [512, 12288], P('row', 'col')
- w1_grad: float32 [4608, 128, 128], P(('row', 'col'))
- w2_grad: float32 [4608, 128, 128], P(('row', 'col'))
The draws below stay inside these ranges and needn't reach their ends.
Inputs may be any that keep to these rules, and one draw needn't show every extreme that they name: Let the device at row index r and col index c hold entries r * 8 + c of the blocks' dimension, 9 of them. Its entries of w1_where name 9 distinct blocks whose block row lies in c * 12 up to (c + 1) * 12 - 1 and whose block column lies in r * 6 up to (r + 1) * 6 - 1; one eighth of the blocks of that region. Likewise the device's entries of w2_where name 9 distinct blocks with block row in r * 6 up to (r + 1) * 6 - 1 and block column in c * 12 up to (c + 1) * 12 - 1.
All inputs are finite; a program needn't handle non-finite values.
Results may differ from the reference program's by a relative error of at most 0.0049.
Values may be sent and summed in bfloat16 or wider, within the bound.
No kernel may reach another device: no remote copies, remote signals or barrier semaphores. Data moves between devices by JAX's collectives and lax.ppermute only.
A program may use at most 64 MiB of HBM per device.

```python
import math
import jax
import jax.numpy as jnp

D = 12288
H = 49152
BS = 128
TOKENS = 512
NBLK = 4608
N_ROW = 64
N_COL = 8
DEVICES = 512


def tile_choice(key):
    subkeys = jax.random.split(key, DEVICES)
    slot_count = D // N_COL // BS * (H // N_ROW // BS)
    picked = NBLK // DEVICES

    def one_device(single):
        middle = 1 + jax.random.permutation(single, slot_count - 2)[:picked - 2]
        ends = jnp.array([0, slot_count - 1], dtype=jnp.int32)
        return jnp.concatenate([ends, middle.astype(jnp.int32)])
    chosen = jax.vmap(one_device)(subkeys)
    return chosen.astype(jnp.int32)


def tile_parts(chosen):
    tile_cols = H // N_ROW // BS
    device = jnp.arange(DEVICES, dtype=jnp.int32)[:, None]
    row_of = device // N_COL
    col_of = device % N_COL
    local_row = chosen // tile_cols
    local_col = chosen % tile_cols
    return (row_of, col_of, local_row, local_col)


def draw_w1_where(key, part):
    key = jax.random.fold_in(key, 11)
    row_of, col_of, local_row, local_col = tile_parts(tile_choice(key))
    tile_rows = D // N_COL // BS
    tile_cols = H // N_ROW // BS
    block_row = col_of * tile_rows + local_row
    block_col = row_of * tile_cols + local_col
    return (block_row * (H // BS) + block_col).reshape(-1).astype(jnp.int32)


def draw_w2_where(key, part):
    key = jax.random.fold_in(key, 23)
    row_of, col_of, local_row, local_col = tile_parts(tile_choice(key))
    tile_rows = D // N_COL // BS
    tile_cols = H // N_ROW // BS
    block_row = row_of * tile_cols + local_col
    block_col = col_of * tile_rows + local_row
    return (block_row * (D // BS) + block_col).reshape(-1).astype(jnp.int32)


def level_of(key, extent, cuts, smallest, largest):
    def one(position, parts):
        heights = jax.random.uniform(jax.random.fold_in(jax.random.fold_in(key, 6), position), (parts,), jnp.float32, smallest / len(cuts), largest / len(cuts))
        return jnp.repeat(jnp.exp(heights), extent[position] // parts).reshape((-1,) + (1,) * (len(extent) - position - 1))

    level = one(*cuts[0])
    for cut in cuts[1:]:
        level = level * one(*cut)
    return level


def normal_values(key, shape, deviation, bound, shards=(), kind=jnp.bfloat16):
    values = deviation * jax.random.normal(key, shape, jnp.float32)
    if shards:
        values = values * level_of(key, shape, shards, -0.22, 0.18)
    return jnp.clip(values, -bound, bound).astype(kind)


def setup_inputs(seed: int = 0) -> dict:
    arg_keys = jax.random.split(jax.random.key(seed), 7)
    return {
        "inputs": normal_values(arg_keys[0], (TOKENS, D), 1.0, 6.0, ((0, 64), (1, 8))),
        "cotangent": normal_values(arg_keys[1], (TOKENS, D), 1.0, 6.0, ((0, 64), (1, 8))),
        "w1_blocks": normal_values(arg_keys[2], (NBLK, BS, BS), (D // 8) ** -0.5, 0.15625, ((0, 512),)),
        "w1_where": draw_w1_where(jax.random.fold_in(arg_keys[6], 71), 0),
        "w2_blocks": normal_values(arg_keys[4], (NBLK, BS, BS), (H // 8) ** -0.5, 0.078125, ((0, 512),)),
        "w2_where": draw_w2_where(jax.random.fold_in(arg_keys[6], 71), 0),
    }


def gelu_value(value):
    inner = math.sqrt(2.0 / math.pi) * (value + 0.044715 * value * value * value)
    return 0.5 * value * (1.0 + jnp.tanh(inner))

def gelu_slope(value):
    inner = math.sqrt(2.0 / math.pi) * (value + 0.044715 * value * value * value)
    tangent = jnp.tanh(inner)
    derive = math.sqrt(2.0 / math.pi) * (1.0 + 3.0 * 0.044715 * value * value)
    return 0.5 * (1.0 + tangent) + 0.5 * value * (1.0 - tangent * tangent) * derive

def apply_blocks(operand, blocks, source, target, width, transpose):
    row_total = operand.shape[0]
    pieces = jnp.take(operand.reshape(row_total, -1, BS).astype(jnp.float32), source, axis=1)
    if transpose:
        product = jnp.einsum('tnm,nkm->ntk', pieces, blocks.astype(jnp.float32))
    else:
        product = jnp.einsum('tnk,nkm->ntm', pieces, blocks.astype(jnp.float32))
    summed = jax.ops.segment_sum(product, target, num_segments=width)
    return jnp.transpose(summed, (1, 0, 2)).reshape(row_total, width * BS)

def block_grads(left_side, right_side, left_index, right_index):
    row_total = left_side.shape[0]
    left_part = jnp.take(left_side.reshape(row_total, -1, BS).astype(jnp.float32), left_index, axis=1)
    right_part = jnp.take(right_side.reshape(row_total, -1, BS).astype(jnp.float32), right_index, axis=1)
    return jnp.einsum('tnk,tnm->nkm', left_part, right_part)

def reference(inputs, cotangent, w1_blocks, w1_where, w2_blocks, w2_where):
    hidden_cols = H // BS
    width_cols = D // BS
    w1_row = (w1_where // hidden_cols).astype(jnp.int32)
    w1_col = (w1_where % hidden_cols).astype(jnp.int32)
    w2_row = (w2_where // width_cols).astype(jnp.int32)
    w2_col = (w2_where % width_cols).astype(jnp.int32)
    hidden = apply_blocks(inputs, w1_blocks, w1_row, w1_col, hidden_cols, False)
    activated = gelu_value(hidden).astype(jnp.bfloat16)
    act_grad = apply_blocks(cotangent, w2_blocks, w2_col, w2_row, hidden_cols, True)
    hidden_grad = (act_grad * gelu_slope(hidden)).astype(jnp.bfloat16)
    input_grad = apply_blocks(hidden_grad, w1_blocks, w1_col, w1_row, width_cols, True).astype(jnp.bfloat16)
    w1_grad = block_grads(inputs, hidden_grad, w1_row, w1_col)
    w2_grad = block_grads(activated, cotangent, w2_row, w2_col)
    return (input_grad, w1_grad, w2_grad)
```

```python
import math

import jax
import jax.numpy as jnp
from jax import lax
from jax.experimental import pallas as pl
from jax.experimental.pallas import tpu as pltpu
from jax.sharding import Mesh, PartitionSpec as P

BF, F32 = jnp.bfloat16, jnp.float32
BS = 128
TOK = 512
WT = 1536
HT = 768
NI = WT // BS
NJ = HT // BS
NB = 9
W1_COLS = 384
W2_COLS = 96
SIZE = {"x": 4, "y": 4, "zh": 4, "zl": 4, "core": 2}
C0 = math.sqrt(2.0 / math.pi)

VM = pl.BlockSpec(memory_space=pltpu.VMEM)
SM = pl.BlockSpec(memory_space=pltpu.SMEM)


def shift(value, axis, step):
    n = SIZE[axis]
    return lax.ppermute(value, axis, [(i, (i + step) % n) for i in range(n)])


def call(body, ins, outs, scratch=(), flops=0, nbytes=0):
    return pl.pallas_call(
        body,
        out_shape=[jax.ShapeDtypeStruct(s, d) for s, d in outs],
        in_specs=[SM if a.dtype == jnp.int32 else VM for a in ins],
        out_specs=[VM] * len(outs),
        scratch_shapes=list(scratch),
        compiler_params=pltpu.CompilerParams(vmem_limit_bytes=40 * 1024 * 1024),
        cost_estimate=pl.CostEstimate(flops=flops, bytes_accessed=nbytes, transcendentals=0),
    )(*ins)


def w1_pos(where):
    return lax.rem(where // W1_COLS, NI), lax.rem(lax.rem(where, W1_COLS), NJ)


def w2_pos(where):
    return lax.rem(lax.rem(where, W2_COLS), NI), lax.rem(where // W2_COLS, NJ)


def lanes(index):
    return pl.ds(pl.multiple_of(index * BS, BS), BS)


NN = (((1,), (0,)), ((), ()))
NT = (((1,), (1,)), ((), ()))
TN = (((0,), (0,)), ((), ()))


def dot(a, b, dims):
    return lax.dot_general(a, b, dims, preferred_element_type=F32)


def partial_body(pos, dims, where, ids, act, blocks, keep, send, acc):
    acc[...] = jnp.zeros_like(acc)
    for b in range(NB):
        i, j = pos(where[b])
        acc[j] += dot(act[:, lanes(i)], blocks[b], dims)
    core = ids[0]
    half = TOK // 2
    mine = pl.ds(pl.multiple_of(core * half, half), half)
    other = pl.ds(pl.multiple_of((1 - core) * half, half), half)
    for j in range(NJ):
        keep[:, j * BS : (j + 1) * BS] = acc[j, mine]
        send[:, j * BS : (j + 1) * BS] = acc[j, other].astype(BF)


def partial_sums(pos, dims, where, ids, act, blocks):
    half = TOK // 2
    return call(
        lambda *refs: partial_body(pos, dims, *refs),
        (where, ids, act, blocks),
        [((half, HT), F32), ((half, HT), BF)],
        [pltpu.VMEM((NJ, TOK, BS), F32)],
        flops=2 * NB * TOK * BS * BS * 4,
        nbytes=3 << 20,
    )


def split_body(ids, keep, got, mine, s1, s2, s3):
    zl = ids[1]
    q = TOK // 8
    own = pl.ds(pl.multiple_of(zl * q, q), q)
    mine[...] = keep[own] + got[own].astype(F32)
    for k, ref in ((1, s1), (2, s2), (3, s3)):
        part = pl.ds(pl.multiple_of(lax.rem(zl + k, 4) * q, q), q)
        ref[...] = (keep[part] + got[part].astype(F32)).astype(BF)


def column_reduce(ids, keep, send):
    got = shift(send, "core", 1)
    q = TOK // 8
    mine, s1, s2, s3 = call(
        split_body,
        (ids, keep, got),
        [((q, HT), F32)] + [((q, HT), BF)] * 3,
        flops=1 << 20,
        nbytes=2 << 20,
    )
    return [mine, shift(s1, "zl", 1), shift(s2, "zl", 2), shift(s3, "zl", 3)]


def gelu_body(h0, h1, h2, h3, a0, a1, a2, a3, activated, hidden_grad):
    v = h0[...] + h1[...].astype(F32) + h2[...].astype(F32) + h3[...].astype(F32)
    g = a0[...] + a1[...].astype(F32) + a2[...].astype(F32) + a3[...].astype(F32)
    t = jnp.tanh(C0 * (v + 0.044715 * v * v * v))
    derive = C0 * (1.0 + 3.0 * 0.044715 * v * v)
    activated[...] = (0.5 * v * (1.0 + t)).astype(BF)
    slope = 0.5 * (1.0 + t) + 0.5 * v * (1.0 - t * t) * derive
    hidden_grad[...] = (g * slope).astype(BF)


def join_body(ids, p0, p1, p2, p3, out):
    zl = ids[1]
    q = TOK // 8
    for k, ref in enumerate((p0, p1, p2, p3)):
        out[pl.ds(pl.multiple_of(lax.rem(zl + 4 - k, 4) * q, q), q)] = ref[...]


def column_gather(ids, piece):
    parts = (piece, shift(piece, "zl", 1), shift(piece, "zl", 2), shift(piece, "zl", 3))
    (own,) = call(join_body, (ids, *parts), [((TOK // 2, HT), BF)], flops=1 << 20, nbytes=1 << 20)
    return own, shift(own, "core", 1)


def whole_tokens(ids, own, got, whole):
    half = TOK // 2
    core = ids[0]
    whole[pl.ds(pl.multiple_of(core * half, half), half)] = own[...]
    whole[pl.ds(pl.multiple_of((1 - core) * half, half), half)] = got[...]


def input_grad_body(where, ids, own, got, blocks, out, whole, acc):
    whole_tokens(ids, own, got, whole)
    acc[...] = jnp.zeros_like(acc)
    for b in range(NB):
        i, j = w1_pos(where[b])
        acc[i] += dot(whole[:, lanes(j)], blocks[b], NT)
    for i in range(NI):
        out[:, i * BS : (i + 1) * BS] = acc[i].astype(BF)


def input_grad_partial(where, ids, own, got, blocks):
    (out,) = call(
        input_grad_body,
        (where, ids, own, got, blocks),
        [((TOK, WT), BF)],
        [pltpu.VMEM((TOK, HT), BF), pltpu.VMEM((NI, TOK, BS), F32)],
        flops=2 * NB * TOK * BS * BS * 4,
        nbytes=4 << 20,
    )
    return out


def block_grad_body(pos, hidden_left, where, ids, own, got, act, out, whole):
    whole_tokens(ids, own, got, whole)
    for b in range(NB):
        i, j = pos(where[b])
        left, right = act[:, lanes(i)], whole[:, lanes(j)]
        if hidden_left:
            left, right = right, left
        out[b] = dot(left, right, TN)


def block_grads(pos, hidden_left, where, ids, own, got, act):
    (out,) = call(
        lambda *refs: block_grad_body(pos, hidden_left, *refs),
        (where, ids, own, got, act),
        [((NB, BS, BS), F32)],
        [pltpu.VMEM((TOK, HT), BF)],
        flops=2 * NB * TOK * BS * BS * 4,
        nbytes=4 << 20,
    )
    return out


def row_gather(shard):
    near = jnp.concatenate([shard] + [shift(shard, "zh", k) for k in (1, 2, 3)], axis=0)
    sixteen = jnp.broadcast_to(near[None], (16, *near.shape)).reshape(TOK, WT)
    return lax.all_to_all(sixteen, ("x", "y"), 0, 0, tiled=True)


def row_reduce(partial):
    parts = lax.all_to_all(partial, ("x", "y"), 0, 0, tiled=True)
    mine = jnp.sum(parts.reshape(16, 4, 8, WT).astype(F32), axis=0)
    sent = mine.astype(BF)
    total = mine[0]
    for k in (1, 2, 3):
        total = total + shift(sent[k], "zh", -k).astype(F32)
    return total.astype(BF)


def shards(inputs, cotangent, w1_blocks, w1_where, w2_blocks, w2_where):
    ids = jnp.stack([lax.axis_index("core"), lax.axis_index("zl")]).astype(jnp.int32)
    whole_inputs = row_gather(inputs)
    whole_cotangent = row_gather(cotangent)
    hidden = column_reduce(ids, *partial_sums(w1_pos, NN, w1_where, ids, whole_inputs, w1_blocks))
    act_grad = column_reduce(
        ids, *partial_sums(w2_pos, NT, w2_where, ids, whole_cotangent, w2_blocks)
    )
    q = TOK // 8
    activated, hidden_grad = call(
        gelu_body, (*hidden, *act_grad), [((q, HT), BF)] * 2, flops=1 << 22, nbytes=1 << 20
    )
    hg = column_gather(ids, hidden_grad)
    partial = input_grad_partial(w1_where, ids, *hg, w1_blocks)
    input_grad = row_reduce(partial)
    av = column_gather(ids, activated)
    w1_grad = block_grads(w1_pos, False, w1_where, ids, *hg, whole_inputs)
    w2_grad = block_grads(w2_pos, True, w2_where, ids, *av, whole_cotangent)
    return input_grad, w1_grad, w2_grad


def solution(mesh):
    fine = Mesh(mesh.devices.reshape(4, 4, 4, 4, 2), ("x", "zh", "y", "zl", "core"))
    row, col = ("x", "zh", "y"), ("zl", "core")
    both = row + col
    return jax.shard_map(
        shards,
        mesh=fine,
        in_specs=(P(row, col), P(row, col), P(both, None, None), P(both), P(both, None, None), P(both)),
        out_specs=(P(row, col), P(both, None, None), P(both, None, None)),
        check_vma=False,
    )
```

```python
import math

import jax
import jax.numpy as jnp
from jax import lax
from jax.experimental import pallas as pl
from jax.experimental.pallas import tpu as pltpu
from jax.sharding import Mesh, PartitionSpec as P

BF, F32 = jnp.bfloat16, jnp.float32
BS = 128
TOK = 512
WT = 1536
HT = 768
NI = WT // BS
NJ = HT // BS
NB = 9
Q = TOK // 8
W1_COLS = 384
W2_COLS = 96
SIZE = {"x": 4, "y": 4, "zh": 4, "zl": 4, "core": 2}
C0 = math.sqrt(2.0 / math.pi)

VM = pl.BlockSpec(memory_space=pltpu.VMEM)
SM = pl.BlockSpec(memory_space=pltpu.SMEM)


def shift(value, axis, step):
    n = SIZE[axis]
    return lax.ppermute(value, axis, [(i, (i + step) % n) for i in range(n)])


def call(body, ins, outs, scratch=(), flops=0, nbytes=0, vmem=16, after=()):
    return pl.pallas_call(
        body,
        out_shape=[jax.ShapeDtypeStruct(s, d) for s, d in outs],
        in_specs=[SM if a.dtype == jnp.int32 else VM for a in ins]
        + [pl.BlockSpec(memory_space=pl.ANY)] * len(after),
        out_specs=[VM] * len(outs),
        scratch_shapes=list(scratch),
        compiler_params=pltpu.CompilerParams(vmem_limit_bytes=vmem << 20),
        cost_estimate=pl.CostEstimate(flops=flops, bytes_accessed=nbytes, transcendentals=0),
    )(*ins, *after)


def w1_pos(where):
    return lax.rem(where // W1_COLS, NI), lax.rem(lax.rem(where, W1_COLS), NJ)


def w2_pos(where):
    return lax.rem(lax.rem(where, W2_COLS), NI), lax.rem(where // W2_COLS, NJ)


def lanes(index):
    return pl.ds(pl.multiple_of(index * BS, BS), BS)


NN = (((1,), (0,)), ((), ()))
NT = (((1,), (1,)), ((), ()))
TN = (((0,), (0,)), ((), ()))


def dot(a, b, dims):
    return lax.dot_general(a, b, dims, preferred_element_type=F32)


def partial_body(pos, dims, pieces, where, ids, *refs):
    core, y = ids[0], ids[2]
    if pieces == 1:
        act, blocks, keep, send, acc = refs
    else:
        parts, (blocks, keep, send, act, acc) = refs[:pieces], refs[pieces:]
        rows = TOK // pieces
        for k, part in enumerate(parts):
            place = lax.rem(y + 4 - k, 4) * rows
            act[pl.ds(pl.multiple_of(place, rows), rows)] = part[...]
    acc[...] = jnp.zeros_like(acc)
    for b in range(NB):
        i, j = pos(where[b])
        acc[j] += dot(act[:, lanes(i)], blocks[b], dims)
    for z in range(4):
        mine = pl.ds(pl.multiple_of((2 * z + core) * Q, Q), Q)
        other = pl.ds(pl.multiple_of((2 * z + 1 - core) * Q, Q), Q)
        for j in range(NJ):
            keep[z * Q : (z + 1) * Q, j * BS : (j + 1) * BS] = acc[j, mine]
            send[z * Q : (z + 1) * Q, j * BS : (j + 1) * BS] = acc[j, other]


def partial_sums(pos, dims, where, ids, parts, blocks):
    half = ((TOK // 2, HT), F32)
    whole = [((TOK, WT), BF)] if len(parts) > 1 else []
    return call(
        lambda *refs: partial_body(pos, dims, len(parts), *refs),
        (where, ids, *parts, blocks),
        [half, half] + whole,
        [pltpu.VMEM((NJ, TOK, BS), F32)],
        flops=2 * NB * TOK * BS * BS * 4,
        nbytes=3 << 20,
    )


def split_body(ids, keep_h, got_h, keep_a, got_a, mine_h, mine_a, s1, s2, s3):
    zl = ids[1]
    own = pl.ds(pl.multiple_of(zl * Q, Q), Q)
    mine_h[...] = keep_h[own] + got_h[own]
    mine_a[...] = keep_a[own] + got_a[own]
    for k, ref in ((1, s1), (2, s2), (3, s3)):
        part = pl.ds(pl.multiple_of(lax.rem(zl + k, 4) * Q, Q), Q)
        ref[:, :HT] = (keep_h[part] + got_h[part]).astype(BF)
        ref[:, HT:] = (keep_a[part] + got_a[part]).astype(BF)


def gelu_body(h0, a0, r1, r2, r3, activated, hidden_grad):
    v, g = h0[...], a0[...]
    for ref in (r1, r2, r3):
        v = v + ref[:, :HT].astype(F32)
        g = g + ref[:, HT:].astype(F32)
    t = jnp.tanh(C0 * (v + 0.044715 * v * v * v))
    derive = C0 * (1.0 + 3.0 * 0.044715 * v * v)
    activated[...] = (0.5 * v * (1.0 + t)).astype(BF)
    slope = 0.5 * (1.0 + t) + 0.5 * v * (1.0 - t * t) * derive
    hidden_grad[...] = (g * slope).astype(BF)


def input_grad_body(where, hg, blocks, out, acc):
    acc[...] = jnp.zeros_like(acc)
    for b in range(NB):
        i, j = w1_pos(where[b])
        acc[i] += dot(hg[:, lanes(j)], blocks[b], NT)
    for i in range(NI):
        out[:, i * BS : (i + 1) * BS] = acc[i].astype(BF)


def input_grad_partial(where, hg, blocks):
    (out,) = call(
        input_grad_body,
        (where, hg, blocks),
        [((TOK, WT), BF)],
        [pltpu.VMEM((NI, TOK, BS), F32)],
        flops=2 * NB * TOK * BS * BS * 4,
        nbytes=4 << 20,
    )
    return out


def block_grad_body(pos, hidden_left, where, hid, act, out):
    for b in range(NB):
        i, j = pos(where[b])
        left, right = act[:, lanes(i)], hid[:, lanes(j)]
        if hidden_left:
            left, right = right, left
        out[b] = dot(left, right, TN)


def block_grads(pos, hidden_left, where, hid, act):
    (out,) = call(
        lambda *refs: block_grad_body(pos, hidden_left, *refs),
        (where, hid, act),
        [((NB, BS, BS), F32)],
        flops=2 * NB * TOK * BS * BS * 4,
        nbytes=4 << 20,
    )
    return out


def sum_body(parts, *refs):
    total = parts[0].astype(F32)
    for k in range(1, 16):
        total = total + parts[k].astype(F32)
    refs[-1][...] = total.astype(BF)


def row_reduce(partial, after):
    parts = lax.all_to_all(partial, ("y", "x"), 0, 0, tiled=True)
    (mine,) = call(
        sum_body,
        (parts.reshape(16, 32, WT),),
        [((32, WT), BF)],
        flops=1 << 20,
        nbytes=2 << 20,
        after=after,
    )
    last = lax.all_to_all(mine, "zh", 0, 0, tiled=True)
    return jnp.sum(last.reshape(4, 8, WT).astype(F32), axis=0).astype(BF)


def shards(inputs, cotangent, w1_blocks, w1_where, w2_blocks, w2_where):
    ids = jnp.stack([lax.axis_index(a) for a in ("core", "zl", "y")]).astype(jnp.int32)
    near = lax.all_gather(jnp.concatenate([inputs, cotangent], axis=0), "zh", axis=0)
    near_inputs = near[:, :8].reshape(32, WT)
    near_cotangent = near[:, 8:].reshape(32, WT)
    sixteen = jnp.broadcast_to(near_inputs[None], (16, 32, WT)).reshape(TOK, WT)
    whole_inputs = lax.all_to_all(sixteen, ("y", "x"), 0, 0, tiled=True)
    along = lax.all_gather(near_cotangent, "x", axis=0, tiled=True)
    quarters = [along] + [shift(along, "y", k) for k in (1, 2, 3)]
    keep_h, send_h = partial_sums(w1_pos, NN, w1_where, ids, [whole_inputs], w1_blocks)
    got_h = shift(send_h, "core", 1)
    keep_a, send_a, whole_cotangent = partial_sums(w2_pos, NT, w2_where, ids, quarters, w2_blocks)
    got_a = shift(send_a, "core", 1)
    mine_h, mine_a, s1, s2, s3 = call(
        split_body,
        (ids, keep_h, got_h, keep_a, got_a),
        [((Q, HT), F32)] * 2 + [((Q, WT), BF)] * 3,
        flops=1 << 20,
        nbytes=2 << 20,
    )
    activated, hidden_grad = call(
        gelu_body,
        (mine_h, mine_a, shift(s1, "zl", 1), shift(s2, "zl", 2), shift(s3, "zl", 3)),
        [((Q, HT), BF)] * 2,
        flops=1 << 22,
        nbytes=1 << 20,
    )
    whole_hg = lax.all_gather(hidden_grad, ("zl", "core"), axis=0, tiled=True)
    whole_av = lax.all_gather(activated, ("zl", "core"), axis=0, tiled=True)
    partial = input_grad_partial(w1_where, whole_hg, w1_blocks)
    w1_grad = block_grads(w1_pos, False, w1_where, whole_hg, whole_inputs)
    w2_grad = block_grads(w2_pos, True, w2_where, whole_av, whole_cotangent)
    input_grad = row_reduce(partial, (whole_av,))
    return input_grad, w1_grad, w2_grad


def solution(mesh):
    fine = Mesh(mesh.devices.reshape(4, 4, 4, 4, 2), ("x", "zh", "y", "zl", "core"))
    row, col = ("x", "zh", "y"), ("zl", "core")
    both = row + col
    return jax.shard_map(
        shards,
        mesh=fine,
        in_specs=(P(row, col), P(row, col), P(both, None, None), P(both), P(both, None, None), P(both)),
        out_specs=(P(row, col), P(both, None, None), P(both, None, None)),
        check_vma=False,
    )
```

```python
import math

import jax
import jax.numpy as jnp
from jax import lax
from jax.experimental import pallas as pl
from jax.experimental.pallas import tpu as pltpu
from jax.sharding import Mesh, PartitionSpec as P

BF, F32 = jnp.bfloat16, jnp.float32
BS = 128
TOK = 512
WT = 1536
HT = 768
NI = WT // BS
NJ = HT // BS
NB = 9
Q = TOK // 8
W1_COLS = 384
W2_COLS = 96
SIZE = {"x": 4, "y": 4, "zh": 4, "zl": 4, "core": 2}
C0 = math.sqrt(2.0 / math.pi)

VM = pl.BlockSpec(memory_space=pltpu.VMEM)
SM = pl.BlockSpec(memory_space=pltpu.SMEM)


def shift(value, axis, step):
    n = SIZE[axis]
    return lax.ppermute(value, axis, [(i, (i + step) % n) for i in range(n)])


def call(body, ins, outs, scratch=(), flops=0, nbytes=0, vmem=16, after=()):
    return pl.pallas_call(
        body,
        out_shape=[jax.ShapeDtypeStruct(s, d) for s, d in outs],
        in_specs=[SM if a.dtype == jnp.int32 else VM for a in ins]
        + [pl.BlockSpec(memory_space=pl.ANY)] * len(after),
        out_specs=[VM] * len(outs),
        scratch_shapes=list(scratch),
        compiler_params=pltpu.CompilerParams(vmem_limit_bytes=vmem << 20),
        cost_estimate=pl.CostEstimate(flops=flops, bytes_accessed=nbytes, transcendentals=0),
    )(*ins, *after)


def w1_pos(where):
    return lax.rem(where // W1_COLS, NI), lax.rem(lax.rem(where, W1_COLS), NJ)


def w2_pos(where):
    return lax.rem(lax.rem(where, W2_COLS), NI), lax.rem(where // W2_COLS, NJ)


def lanes(index):
    return pl.ds(pl.multiple_of(index * BS, BS), BS)


NN = (((1,), (0,)), ((), ()))
NT = (((1,), (1,)), ((), ()))
TN = (((0,), (0,)), ((), ()))


def dot(a, b, dims):
    return lax.dot_general(a, b, dims, preferred_element_type=F32)


def rows_of(parts, first, index):
    return parts[:, first : first + 32, lanes(index)].reshape(TOK, BS)


def partial_body(where1, where2, ids, parts, blocks1, blocks2, keep, send, acc):
    core = ids[0]
    acc[...] = jnp.zeros_like(acc)
    for b in range(NB):
        i, j = w1_pos(where1[b])
        acc[j] += dot(rows_of(parts, 0, i), blocks1[b], NN)
        i, j = w2_pos(where2[b])
        acc[NJ + j] += dot(rows_of(parts, 32, i), blocks2[b], NT)
    for z in range(4):
        mine = pl.ds(pl.multiple_of((2 * z + core) * Q, Q), Q)
        other = pl.ds(pl.multiple_of((2 * z + 1 - core) * Q, Q), Q)
        for j in range(2 * NJ):
            keep[z * Q : (z + 1) * Q, j * BS : (j + 1) * BS] = acc[j, mine]
            send[z * Q : (z + 1) * Q, j * BS : (j + 1) * BS] = acc[j, other]


def split_body(ids, keep, got, mine, s1, s2, s3):
    zl = ids[1]
    own = pl.ds(pl.multiple_of(zl * Q, Q), Q)
    mine[...] = keep[own] + got[own]
    for k, ref in ((1, s1), (2, s2), (3, s3)):
        part = pl.ds(pl.multiple_of(lax.rem(zl + k, 4) * Q, Q), Q)
        ref[...] = (keep[part] + got[part]).astype(BF)


def gelu_body(own, r1, r2, r3, activated, hidden_grad):
    v, g = own[:, :HT], own[:, HT:]
    for ref in (r1, r2, r3):
        v = v + ref[:, :HT].astype(F32)
        g = g + ref[:, HT:].astype(F32)
    t = jnp.tanh(C0 * (v + 0.044715 * v * v * v))
    derive = C0 * (1.0 + 3.0 * 0.044715 * v * v)
    activated[...] = (0.5 * v * (1.0 + t)).astype(BF)
    slope = 0.5 * (1.0 + t) + 0.5 * v * (1.0 - t * t) * derive
    hidden_grad[...] = (g * slope).astype(BF)


def input_grad_body(where, hg, blocks, out, acc):
    acc[...] = jnp.zeros_like(acc)
    for b in range(NB):
        i, j = w1_pos(where[b])
        acc[i] += dot(hg[:, lanes(j)], blocks[b], NT)
    for i in range(NI):
        out[:, i * BS : (i + 1) * BS] = acc[i].astype(BF)


def input_grad_partial(where, hg, blocks):
    (out,) = call(
        input_grad_body,
        (where, hg, blocks),
        [((TOK, WT), BF)],
        [pltpu.VMEM((NI, TOK, BS), F32)],
        flops=2 * NB * TOK * BS * BS * 4,
        nbytes=4 << 20,
    )
    return out


def block_grad_body(pos, first, where, hid, parts, out):
    for b in range(NB):
        i, j = pos(where[b])
        left, right = rows_of(parts, first, i), hid[:, lanes(j)]
        if first:
            left, right = right, left
        out[b] = dot(left, right, TN)


def block_grads(pos, first, where, hid, parts):
    (out,) = call(
        lambda *refs: block_grad_body(pos, first, *refs),
        (where, hid, parts),
        [((NB, BS, BS), F32)],
        flops=2 * NB * TOK * BS * BS * 4,
        nbytes=4 << 20,
    )
    return out


def sum_body(parts, *refs):
    total = parts[0].astype(F32)
    for k in range(1, 16):
        total = total + parts[k].astype(F32)
    refs[-1][...] = total.astype(BF)


def row_reduce(partial, after):
    parts = lax.all_to_all(partial, ("y", "x"), 0, 0, tiled=True)
    (mine,) = call(
        sum_body,
        (parts.reshape(16, 32, WT),),
        [((32, WT), BF)],
        flops=1 << 20,
        nbytes=2 << 20,
        after=after,
    )
    last = lax.all_to_all(mine, "zh", 0, 0, tiled=True)
    return jnp.sum(last.reshape(4, 8, WT).astype(F32), axis=0).astype(BF)


def shards(inputs, cotangent, w1_blocks, w1_where, w2_blocks, w2_where):
    ids = jnp.stack([lax.axis_index(a) for a in ("core", "zl")]).astype(jnp.int32)
    near = lax.all_gather(jnp.concatenate([inputs, cotangent], axis=0), "zh", axis=0)
    near = near.reshape(4, 2, 8, WT).swapaxes(0, 1).reshape(64, WT)
    sixteen = jnp.broadcast_to(near[None], (16, 64, WT))
    parts = lax.all_to_all(sixteen, ("y", "x"), 0, 0, tiled=True)
    keep, send = call(
        partial_body,
        (w1_where, w2_where, ids, parts, w1_blocks, w2_blocks),
        [((TOK // 2, WT), F32)] * 2,
        [pltpu.VMEM((2 * NJ, TOK, BS), F32)],
        flops=2 * NB * TOK * BS * BS * 8,
        nbytes=6 << 20,
        vmem=24,
    )
    mine, s1, s2, s3 = call(
        split_body,
        (ids, keep, shift(send, "core", 1)),
        [((Q, WT), F32)] + [((Q, WT), BF)] * 3,
        flops=1 << 20,
        nbytes=2 << 20,
    )
    activated, hidden_grad = call(
        gelu_body,
        (mine, shift(s1, "zl", 1), shift(s2, "zl", 2), shift(s3, "zl", 3)),
        [((Q, HT), BF)] * 2,
        flops=1 << 22,
        nbytes=1 << 20,
    )
    whole_hg = lax.all_gather(hidden_grad, ("zl", "core"), axis=0, tiled=True)
    whole_av = lax.all_gather(activated, ("zl", "core"), axis=0, tiled=True)
    partial = input_grad_partial(w1_where, whole_hg, w1_blocks)
    w1_grad = block_grads(w1_pos, 0, w1_where, whole_hg, parts)
    w2_grad = block_grads(w2_pos, 32, w2_where, whole_av, parts)
    input_grad = row_reduce(partial, (whole_av[:16, :BS],))
    return input_grad, w1_grad, w2_grad


def solution(mesh):
    fine = Mesh(mesh.devices.reshape(4, 4, 4, 4, 2), ("x", "zh", "y", "zl", "core"))
    row, col = ("x", "zh", "y"), ("zl", "core")
    both = row + col
    return jax.shard_map(
        shards,
        mesh=fine,
        in_specs=(P(row, col), P(row, col), P(both, None, None), P(both), P(both, None, None), P(both)),
        out_specs=(P(row, col), P(both, None, None), P(both, None, None)),
        check_vma=False,
    )
```

```python
import math

import jax
import jax.numpy as jnp
from jax import lax
from jax.experimental import pallas as pl
from jax.experimental.pallas import tpu as pltpu
from jax.sharding import Mesh, PartitionSpec as P

BF, F32 = jnp.bfloat16, jnp.float32
BS = 128
TOK = 512
WT = 1536
HT = 768
NI = WT // BS
NJ = HT // BS
NB = 9
Q = TOK // 8
STEPS = (0, 1, 3, 2)
FIRST = 3 * Q // 4
W1_COLS = 384
W2_COLS = 96
SIZE = {"x": 4, "y": 4, "zh": 4, "zl": 4, "core": 2}
C0 = math.sqrt(2.0 / math.pi)

VM = pl.BlockSpec(memory_space=pltpu.VMEM)
SM = pl.BlockSpec(memory_space=pltpu.SMEM)


def shift(value, axis, step):
    n = SIZE[axis]
    return lax.ppermute(value, axis, [(i, (i + step) % n) for i in range(n)])


def call(body, ins, outs, scratch=(), flops=0, nbytes=0, vmem=16, after=()):
    n, m = len(ins), len(ins) + len(after)
    return pl.pallas_call(
        lambda *refs: body(*refs[:n], *refs[m:]),
        out_shape=[jax.ShapeDtypeStruct(s, d) for s, d in outs],
        in_specs=[SM if a.dtype == jnp.int32 else VM for a in ins]
        + [pl.BlockSpec(memory_space=pl.ANY)] * len(after),
        out_specs=[VM] * len(outs),
        scratch_shapes=list(scratch),
        compiler_params=pltpu.CompilerParams(vmem_limit_bytes=vmem << 20),
        cost_estimate=pl.CostEstimate(flops=flops, bytes_accessed=nbytes, transcendentals=0),
    )(*ins, *after)


def w1_pos(where):
    return lax.rem(where // W1_COLS, NI), lax.rem(lax.rem(where, W1_COLS), NJ)


def w2_pos(where):
    return lax.rem(lax.rem(where, W2_COLS), NI), lax.rem(where // W2_COLS, NJ)


def lanes(index):
    return pl.ds(pl.multiple_of(index * BS, BS), BS)


NN = (((1,), (0,)), ((), ()))
NT = (((1,), (1,)), ((), ()))
TN = (((0,), (0,)), ((), ()))


def dot(a, b, dims):
    return lax.dot_general(a, b, dims, preferred_element_type=F32)


def rows_of(parts, first, index):
    at = lanes(index)
    return jnp.concatenate([p[:, first : first + 32, at].reshape(4 * 32, BS) for p in parts], axis=0)


def partial_body(where1, where2, ids, *refs):
    parts, (blocks1, blocks2, keep, send, acc) = refs[:-5], refs[-5:]
    n = len(parts) * 16
    core = ids[0]
    acc[...] = jnp.zeros_like(acc)
    for b in range(NB):
        i, j = w1_pos(where1[b])
        acc[j] += dot(rows_of(parts, 0, i), blocks1[b], NN)
        i, j = w2_pos(where2[b])
        acc[NJ + j] += dot(rows_of(parts, 32, i), blocks2[b], NT)
    for z in range(4):
        mine = pl.ds(pl.multiple_of((2 * z + core) * n, n), n)
        other = pl.ds(pl.multiple_of((2 * z + 1 - core) * n, n), n)
        for j in range(2 * NJ):
            keep[z * n : (z + 1) * n, j * BS : (j + 1) * BS] = acc[j, mine]
            send[z * n : (z + 1) * n, j * BS : (j + 1) * BS] = acc[j, other]


def split_body(ids, keep, got, mine, s1, s2, s3):
    n = mine.shape[0]
    zl = ids[1]
    own = pl.ds(pl.multiple_of(zl * n, n), n)
    mine[...] = keep[own] + got[own]
    for k, ref in ((1, s1), (2, s2), (3, s3)):
        part = pl.ds(pl.multiple_of(lax.rem(zl + k, 4) * n, n), n)
        ref[...] = (keep[part] + got[part]).astype(BF)


def product_terms(ids, where1, where2, parts, blocks1, blocks2, after=()):
    n = len(parts)
    return call(
        partial_body,
        (where1, where2, ids, *parts, blocks1, blocks2),
        [((n * Q, WT), F32)] * 2,
        [pltpu.VMEM((2 * NJ, n * 128, BS), F32)],
        flops=2 * NB * n * 128 * BS * BS * 8,
        nbytes=n << 21,
        after=after,
        vmem=20,
    )


def column_sums(ids, keep, got):
    n = keep.shape[0] // 4
    mine, s1, s2, s3 = call(
        split_body,
        (ids, keep, got),
        [((n, WT), F32)] + [((n, WT), BF)] * 3,
        flops=1 << 20,
        nbytes=1 << 20,
    )
    return mine, shift(s1, "zl", 1), shift(s2, "zl", 2), shift(s3, "zl", 3)


def gelu_body(*refs):
    activated, hidden_grad = refs[8:]
    for h in range(2):
        own, r1, r2, r3 = refs[4 * h : 4 * h + 4]
        v, g = own[:, :HT], own[:, HT:]
        for ref in (r1, r2, r3):
            v = v + ref[:, :HT].astype(F32)
            g = g + ref[:, HT:].astype(F32)
        t = jnp.tanh(C0 * (v + 0.044715 * v * v * v))
        derive = C0 * (1.0 + 3.0 * 0.044715 * v * v)
        slope = 0.5 * (1.0 + t) + 0.5 * v * (1.0 - t * t) * derive
        at = slice(0, FIRST) if h == 0 else slice(FIRST, Q)
        activated[at] = (0.5 * v * (1.0 + t)).astype(BF)
        hidden_grad[at] = (g * slope).astype(BF)


def tokens_of(hid, index):
    at = lanes(index)
    return jnp.concatenate(
        [hid[:, :FIRST, at].reshape(8 * FIRST, BS), hid[:, FIRST:, at].reshape(8 * (Q - FIRST), BS)], axis=0
    )


def input_grad_body(where, ids, hg, blocks, out, acc):
    y = ids[2]
    acc[...] = jnp.zeros_like(acc)
    for b in range(NB):
        i, j = w1_pos(where[b])
        acc[i] += dot(tokens_of(hg, j), blocks[b], NT)
    for q, step in enumerate(STEPS):
        owner = lax.rem(y + 4 - step, 4) * 4
        for x in range(4):
            row = (4 * q + x) * 32
            for i in range(NI):
                out[owner + x, :, i * BS : (i + 1) * BS] = acc[i, row : row + 32].astype(BF)


def input_grad_partial(where, ids, hg, blocks):
    (out,) = call(
        input_grad_body,
        (where, ids, hg, blocks),
        [((16, 32, WT), BF)],
        [pltpu.VMEM((NI, TOK, BS), F32)],
        flops=2 * NB * TOK * BS * BS * 4,
        nbytes=4 << 20,
    )
    return out


def block_grad_body(pos, first, where, hid, *refs):
    parts, out = refs[:4], refs[4]
    for b in range(NB):
        i, j = pos(where[b])
        left, right = rows_of(parts, first, i), tokens_of(hid, j)
        if first:
            left, right = right, left
        out[b] = dot(left, right, TN)


def block_grads(pos, first, where, hid, parts):
    (out,) = call(
        lambda *refs: block_grad_body(pos, first, *refs),
        (where, hid, *parts),
        [((NB, BS, BS), F32)],
        flops=2 * NB * TOK * BS * BS * 4,
        nbytes=4 << 20,
    )
    return out


def sum_body(parts, out):
    total = parts[0].astype(F32)
    for k in range(1, 16):
        total = total + parts[k].astype(F32)
    out[...] = total.astype(BF)


def row_reduce(partial, after):
    parts = lax.all_to_all(partial, ("y", "x"), 0, 0, tiled=True)
    (mine,) = call(
        sum_body,
        (parts,),
        [((32, WT), BF)],
        flops=1 << 20,
        nbytes=2 << 20,
        after=after,
    )
    last = lax.all_to_all(mine, "zh", 0, 0, tiled=True)
    return jnp.sum(last.reshape(4, 8, WT).astype(F32), axis=0).astype(BF)


def shards(inputs, cotangent, w1_blocks, w1_where, w2_blocks, w2_where):
    ids = jnp.stack([lax.axis_index(a) for a in ("core", "zl", "y")]).astype(jnp.int32)
    near = lax.all_gather(jnp.concatenate([inputs, cotangent], axis=0), "zh", axis=0)
    near = near.reshape(4, 2, 8, WT).swapaxes(0, 1).reshape(64, WT)
    along = lax.all_gather(near, "x", axis=0)
    parts = [along, shift(along, "y", 1), shift(along, "y", 3)]
    weights = (w1_blocks, w2_blocks)
    parts.append(shift(along, "y", 2))
    keep, send = product_terms(ids, w1_where, w2_where, parts[:3], *weights)
    first = column_sums(ids, keep, shift(send, "core", 1))
    keep, send = product_terms(ids, w1_where, w2_where, parts[3:], *weights, after=first[1:])
    second = column_sums(ids, keep, shift(send, "core", 1))
    activated, hidden_grad = call(
        gelu_body, (*first, *second), [((Q, HT), BF)] * 2, flops=1 << 22, nbytes=1 << 20
    )
    whole_hg = lax.all_gather(hidden_grad, ("zl", "core"), axis=0, tiled=True).reshape(8, Q, HT)
    whole_av = lax.all_gather(activated, ("zl", "core"), axis=0, tiled=True).reshape(8, Q, HT)
    partial = input_grad_partial(w1_where, ids, whole_hg, w1_blocks)
    w1_grad = block_grads(w1_pos, 0, w1_where, whole_hg, parts)
    w2_grad = block_grads(w2_pos, 32, w2_where, whole_av, parts)
    input_grad = row_reduce(partial, (whole_av[0, :16, :BS],))
    return input_grad, w1_grad, w2_grad


def solution(mesh):
    fine = Mesh(mesh.devices.reshape(4, 4, 4, 4, 2), ("x", "zh", "y", "zl", "core"))
    row, col = ("x", "zh", "y"), ("zl", "core")
    both = row + col
    return jax.shard_map(
        shards,
        mesh=fine,
        in_specs=(P(row, col), P(row, col), P(both, None, None), P(both), P(both, None, None), P(both)),
        out_specs=(P(row, col), P(both, None, None), P(both, None, None)),
        check_vma=False,
    )
```

```python
import math

import jax
import jax.numpy as jnp
from jax import lax
from jax.experimental import pallas as pl
from jax.experimental.pallas import tpu as pltpu
from jax.sharding import Mesh, PartitionSpec as P

BF, F32 = jnp.bfloat16, jnp.float32
BS = 128
TOK = 512
WT = 1536
HT = 768
NI = WT // BS
NJ = HT // BS
NB = 9
Q = TOK // 8
STEPS = (0, 1, 3, 2)
FIRST = Q // 4
W1_COLS = 384
W2_COLS = 96
SIZE = {"x": 4, "y": 4, "zh": 4, "zl": 4, "core": 2}
C0 = math.sqrt(2.0 / math.pi)

VM = pl.BlockSpec(memory_space=pltpu.VMEM)
SM = pl.BlockSpec(memory_space=pltpu.SMEM)


def shift(value, axis, step):
    n = SIZE[axis]
    return lax.ppermute(value, axis, [(i, (i + step) % n) for i in range(n)])


def call(body, ins, outs, scratch=(), flops=0, nbytes=0, vmem=16, after=()):
    n, m = len(ins), len(ins) + len(after)
    return pl.pallas_call(
        lambda *refs: body(*refs[:n], *refs[m:]),
        out_shape=[jax.ShapeDtypeStruct(s, d) for s, d in outs],
        in_specs=[SM if a.dtype == jnp.int32 else VM for a in ins]
        + [pl.BlockSpec(memory_space=pl.ANY)] * len(after),
        out_specs=[VM] * len(outs),
        scratch_shapes=list(scratch),
        compiler_params=pltpu.CompilerParams(vmem_limit_bytes=vmem << 20),
        cost_estimate=pl.CostEstimate(flops=flops, bytes_accessed=nbytes, transcendentals=0),
    )(*ins, *after)


def w1_pos(where):
    return lax.rem(where // W1_COLS, NI), lax.rem(lax.rem(where, W1_COLS), NJ)


def w2_pos(where):
    return lax.rem(lax.rem(where, W2_COLS), NI), lax.rem(where // W2_COLS, NJ)


def lanes(index):
    return pl.ds(pl.multiple_of(index * BS, BS), BS)


NN = (((1,), (0,)), ((), ()))
NT = (((1,), (1,)), ((), ()))
TN = (((0,), (0,)), ((), ()))


def dot(a, b, dims):
    return lax.dot_general(a, b, dims, preferred_element_type=F32)


def rows_of(parts, first, index):
    at = lanes(index)
    return jnp.concatenate([p[:, first : first + 32, at].reshape(4 * 32, BS) for p in parts], axis=0)


def partial_body(where1, where2, ids, *refs):
    parts, (blocks1, blocks2, keep, send, acc) = refs[:-5], refs[-5:]
    n = len(parts) * 16
    core = ids[0]
    acc[...] = jnp.zeros_like(acc)
    for b in range(NB):
        i, j = w1_pos(where1[b])
        acc[j] += dot(rows_of(parts, 0, i), blocks1[b], NN)
        i, j = w2_pos(where2[b])
        acc[NJ + j] += dot(rows_of(parts, 32, i), blocks2[b], NT)
    for z in range(4):
        mine = pl.ds(pl.multiple_of((2 * z + core) * n, n), n)
        other = pl.ds(pl.multiple_of((2 * z + 1 - core) * n, n), n)
        for j in range(2 * NJ):
            keep[z * n : (z + 1) * n, j * BS : (j + 1) * BS] = acc[j, mine]
            send[z * n : (z + 1) * n, j * BS : (j + 1) * BS] = acc[j, other]


def split_body(ids, keep, got, mine, s1, s2, s3):
    n = mine.shape[0]
    zl = ids[1]
    own = pl.ds(pl.multiple_of(zl * n, n), n)
    mine[...] = keep[own] + got[own]
    for k, ref in ((1, s1), (2, s2), (3, s3)):
        part = pl.ds(pl.multiple_of(lax.rem(zl + k, 4) * n, n), n)
        ref[...] = (keep[part] + got[part]).astype(BF)


def product_terms(ids, where1, where2, parts, blocks1, blocks2, after=()):
    n = len(parts)
    return call(
        partial_body,
        (where1, where2, ids, *parts, blocks1, blocks2),
        [((n * Q, WT), F32)] * 2,
        [pltpu.VMEM((2 * NJ, n * 128, BS), F32)],
        flops=2 * NB * n * 128 * BS * BS * 8,
        nbytes=n << 21,
        after=after,
        vmem=20,
    )


def column_sums(ids, keep, got):
    n = keep.shape[0] // 4
    mine, s1, s2, s3 = call(
        split_body,
        (ids, keep, got),
        [((n, WT), F32)] + [((n, WT), BF)] * 3,
        flops=1 << 20,
        nbytes=1 << 20,
    )
    return mine, shift(s1, "zl", 1), shift(s2, "zl", 2), shift(s3, "zl", 3)


def gelu_body(*refs):
    activated, hidden_grad = refs[8:]
    for h in range(2):
        own, r1, r2, r3 = refs[4 * h : 4 * h + 4]
        v, g = own[:, :HT], own[:, HT:]
        for ref in (r1, r2, r3):
            v = v + ref[:, :HT].astype(F32)
            g = g + ref[:, HT:].astype(F32)
        t = jnp.tanh(C0 * (v + 0.044715 * v * v * v))
        derive = C0 * (1.0 + 3.0 * 0.044715 * v * v)
        slope = 0.5 * (1.0 + t) + 0.5 * v * (1.0 - t * t) * derive
        at = slice(0, FIRST) if h == 0 else slice(FIRST, Q)
        activated[at] = (0.5 * v * (1.0 + t)).astype(BF)
        hidden_grad[at] = (g * slope).astype(BF)


def tokens_of(hid, index):
    at = lanes(index)
    return jnp.concatenate(
        [hid[:, :FIRST, at].reshape(8 * FIRST, BS), hid[:, FIRST:, at].reshape(8 * (Q - FIRST), BS)], axis=0
    )


def input_grad_body(where, ids, hg, blocks, out, acc):
    y = ids[2]
    acc[...] = jnp.zeros_like(acc)
    for b in range(NB):
        i, j = w1_pos(where[b])
        acc[i] += dot(tokens_of(hg, j), blocks[b], NT)
    for q, step in enumerate(STEPS):
        owner = lax.rem(y + 4 - step, 4) * 4
        for x in range(4):
            row = (4 * q + x) * 32
            for i in range(NI):
                out[owner + x, :, i * BS : (i + 1) * BS] = acc[i, row : row + 32].astype(BF)


def input_grad_partial(where, ids, hg, blocks):
    (out,) = call(
        input_grad_body,
        (where, ids, hg, blocks),
        [((16, 32, WT), BF)],
        [pltpu.VMEM((NI, TOK, BS), F32)],
        flops=2 * NB * TOK * BS * BS * 4,
        nbytes=4 << 20,
    )
    return out


def block_grad_body(pos, first, where, hid, *refs):
    parts, out = refs[:4], refs[4]
    for b in range(NB):
        i, j = pos(where[b])
        left, right = rows_of(parts, first, i), tokens_of(hid, j)
        if first:
            left, right = right, left
        out[b] = dot(left, right, TN)


def block_grads(pos, first, where, hid, parts):
    (out,) = call(
        lambda *refs: block_grad_body(pos, first, *refs),
        (where, hid, *parts),
        [((NB, BS, BS), F32)],
        flops=2 * NB * TOK * BS * BS * 4,
        nbytes=4 << 20,
    )
    return out


def sum_body(parts, out):
    total = parts[0].astype(F32)
    for k in range(1, 16):
        total = total + parts[k].astype(F32)
    out[...] = total.astype(BF)


def row_reduce(partial, after):
    parts = lax.all_to_all(partial, ("y", "x"), 0, 0, tiled=True)
    (mine,) = call(
        sum_body,
        (parts,),
        [((32, WT), BF)],
        flops=1 << 20,
        nbytes=2 << 20,
        after=after,
    )
    last = lax.all_to_all(mine, "zh", 0, 0, tiled=True)
    return jnp.sum(last.reshape(4, 8, WT).astype(F32), axis=0).astype(BF)


def shards(inputs, cotangent, w1_blocks, w1_where, w2_blocks, w2_where):
    ids = jnp.stack([lax.axis_index(a) for a in ("core", "zl", "y")]).astype(jnp.int32)
    near = lax.all_gather(jnp.concatenate([inputs, cotangent], axis=0), "zh", axis=0)
    near = near.reshape(4, 2, 8, WT).swapaxes(0, 1).reshape(64, WT)
    along = lax.all_gather(near, "x", axis=0)
    parts = [along] + [shift(along, "y", step) for step in STEPS[1:]]
    weights = (w1_blocks, w2_blocks)
    keep, send = product_terms(ids, w1_where, w2_where, parts[:1], *weights)
    first = column_sums(ids, keep, shift(send, "core", 1))
    keep, send = product_terms(ids, w1_where, w2_where, parts[1:], *weights, after=first[1:])
    second = column_sums(ids, keep, shift(send, "core", 1))
    activated, hidden_grad = call(
        gelu_body, (*first, *second), [((Q, HT), BF)] * 2, flops=1 << 22, nbytes=1 << 20
    )
    whole_hg = lax.all_gather(hidden_grad, ("zl", "core"), axis=0, tiled=True).reshape(8, Q, HT)
    whole_av = lax.all_gather(activated, ("zl", "core"), axis=0, tiled=True).reshape(8, Q, HT)
    partial = input_grad_partial(w1_where, ids, whole_hg, w1_blocks)
    w1_grad = block_grads(w1_pos, 0, w1_where, whole_hg, parts)
    w2_grad = block_grads(w2_pos, 32, w2_where, whole_av, parts)
    input_grad = row_reduce(partial, (whole_av[0, :16, :BS],))
    return input_grad, w1_grad, w2_grad


def solution(mesh):
    fine = Mesh(mesh.devices.reshape(4, 4, 4, 4, 2), ("x", "zh", "y", "zl", "core"))
    row, col = ("x", "zh", "y"), ("zl", "core")
    both = row + col
    return jax.shard_map(
        shards,
        mesh=fine,
        in_specs=(P(row, col), P(row, col), P(both, None, None), P(both), P(both, None, None), P(both)),
        out_specs=(P(row, col), P(both, None, None), P(both, None, None)),
        check_vma=False,
    )
```

```python
import math

import jax
import jax.numpy as jnp
from jax import lax
from jax.experimental import pallas as pl
from jax.experimental.pallas import tpu as pltpu
from jax.sharding import Mesh, PartitionSpec as P

BF, F32 = jnp.bfloat16, jnp.float32
BS = 128
TOK = 512
WT = 1536
HT = 768
NI = WT // BS
NJ = HT // BS
NB = 9
Q = TOK // 8
STEPS = (0, 1, 3, 2)
FIRST = Q // 4
W1_COLS = 384
W2_COLS = 96
SIZE = {"x": 4, "y": 4, "zh": 4, "zl": 4, "core": 2}
C0 = math.sqrt(2.0 / math.pi)

VM = pl.BlockSpec(memory_space=pltpu.VMEM)
SM = pl.BlockSpec(memory_space=pltpu.SMEM)


def shift(value, axis, step):
    n = SIZE[axis]
    return lax.ppermute(value, axis, [(i, (i + step) % n) for i in range(n)])


def call(body, ins, outs, scratch=(), flops=0, nbytes=0, vmem=16, after=(), out_space=pltpu.VMEM):
    n, m = len(ins), len(ins) + len(after)
    shape = pltpu.HBM if out_space == pltpu.HBM else jax.ShapeDtypeStruct
    return pl.pallas_call(
        lambda *refs: body(*refs[:n], *refs[m:]),
        out_shape=[shape(s, d) for s, d in outs],
        in_specs=[SM if a.dtype == jnp.int32 else VM for a in ins]
        + [pl.BlockSpec(memory_space=pl.ANY)] * len(after),
        out_specs=[pl.BlockSpec(memory_space=out_space)] * len(outs),
        scratch_shapes=list(scratch),
        compiler_params=pltpu.CompilerParams(vmem_limit_bytes=vmem << 20),
        cost_estimate=pl.CostEstimate(flops=flops, bytes_accessed=nbytes, transcendentals=0),
    )(*ins, *after)


def w1_pos(where):
    return lax.rem(where // W1_COLS, NI), lax.rem(lax.rem(where, W1_COLS), NJ)


def w2_pos(where):
    return lax.rem(lax.rem(where, W2_COLS), NI), lax.rem(where // W2_COLS, NJ)


def lanes(index):
    return pl.ds(pl.multiple_of(index * BS, BS), BS)


NN = (((1,), (0,)), ((), ()))
NT = (((1,), (1,)), ((), ()))
TN = (((0,), (0,)), ((), ()))


def dot(a, b, dims):
    return lax.dot_general(a, b, dims, preferred_element_type=F32)


def rows_of(parts, first, index):
    at = lanes(index)
    return jnp.concatenate([p[:, first : first + 32, at].reshape(4 * 32, BS) for p in parts], axis=0)


def partial_body(where1, where2, ids, *refs):
    parts, (blocks1, blocks2, keep, send, acc) = refs[:-5], refs[-5:]
    n = len(parts) * 16
    core = ids[0]
    acc[...] = jnp.zeros_like(acc)
    for b in range(NB):
        i, j = w1_pos(where1[b])
        acc[j] += dot(rows_of(parts, 0, i), blocks1[b], NN)
        i, j = w2_pos(where2[b])
        acc[NJ + j] += dot(rows_of(parts, 32, i), blocks2[b], NT)
    for z in range(4):
        mine = pl.ds(pl.multiple_of((2 * z + core) * n, n), n)
        other = pl.ds(pl.multiple_of((2 * z + 1 - core) * n, n), n)
        for j in range(2 * NJ):
            keep[z * n : (z + 1) * n, j * BS : (j + 1) * BS] = acc[j, mine]
            send[z * n : (z + 1) * n, j * BS : (j + 1) * BS] = acc[j, other]


def split_body(ids, keep, got, mine, s1, s2, s3):
    n = mine.shape[0]
    zl = ids[1]
    own = pl.ds(pl.multiple_of(zl * n, n), n)
    mine[...] = keep[own] + got[own]
    for k, ref in ((1, s1), (2, s2), (3, s3)):
        part = pl.ds(pl.multiple_of(lax.rem(zl + k, 4) * n, n), n)
        ref[...] = (keep[part] + got[part]).astype(BF)


def product_terms(ids, where1, where2, parts, blocks1, blocks2, after=()):
    n = len(parts)
    return call(
        partial_body,
        (where1, where2, ids, *parts, blocks1, blocks2),
        [((n * Q, WT), F32)] * 2,
        [pltpu.VMEM((2 * NJ, n * 128, BS), F32)],
        flops=2 * NB * n * 128 * BS * BS * 8,
        nbytes=n << 21,
        after=after,
        vmem=20,
    )


def column_sums(ids, keep, got):
    n = keep.shape[0] // 4
    mine, s1, s2, s3 = call(
        split_body,
        (ids, keep, got),
        [((n, WT), F32)] + [((n, WT), BF)] * 3,
        flops=1 << 20,
        nbytes=1 << 20,
    )
    return mine, shift(s1, "zl", 1), shift(s2, "zl", 2), shift(s3, "zl", 3)


def gelu_body(*refs):
    activated, hidden_grad = refs[8:]
    for h in range(2):
        own, r1, r2, r3 = refs[4 * h : 4 * h + 4]
        v, g = own[:, :HT], own[:, HT:]
        for ref in (r1, r2, r3):
            v = v + ref[:, :HT].astype(F32)
            g = g + ref[:, HT:].astype(F32)
        t = jnp.tanh(C0 * (v + 0.044715 * v * v * v))
        derive = C0 * (1.0 + 3.0 * 0.044715 * v * v)
        slope = 0.5 * (1.0 + t) + 0.5 * v * (1.0 - t * t) * derive
        at = slice(0, FIRST) if h == 0 else slice(FIRST, Q)
        activated[at] = (0.5 * v * (1.0 + t)).astype(BF)
        hidden_grad[at] = (g * slope).astype(BF)


def tokens_of(hid, index):
    at = lanes(index)
    return jnp.concatenate(
        [hid[:, :FIRST, at].reshape(8 * FIRST, BS), hid[:, FIRST:, at].reshape(8 * (Q - FIRST), BS)], axis=0
    )


def input_grad_body(where, ids, hg, blocks, out, acc, staged, sems):
    y = ids[2]
    acc[...] = jnp.zeros_like(acc)
    for b in range(NB):
        i, j = w1_pos(where[b])
        acc[i] += dot(tokens_of(hg, j), blocks[b], NT)
    copies = []
    for q, step in enumerate(STEPS):
        for x in range(4):
            row = (4 * q + x) * 32
            for i in range(NI):
                staged[4 * q + x, :, i * BS : (i + 1) * BS] = acc[i, row : row + 32].astype(BF)
        owner = lax.rem(y + 4 - step, 4) * 4
        copies.append(
            pltpu.make_async_copy(staged.at[pl.ds(4 * q, 4)], out.at[pl.ds(owner, 4)], sems.at[q])
        )
        copies[-1].start()
    for copy in copies:
        copy.wait()


def input_grad_partial(where, ids, hg, blocks):
    (out,) = call(
        input_grad_body,
        (where, ids, hg, blocks),
        [((16, 32, WT), BF)],
        [
            pltpu.VMEM((NI, TOK, BS), F32),
            pltpu.VMEM((16, 32, WT), BF),
            pltpu.SemaphoreType.DMA((4,)),
        ],
        out_space=pltpu.HBM,
        flops=2 * NB * TOK * BS * BS * 4,
        nbytes=4 << 20,
    )
    return out


def block_grad_body(pos, first, where, hid, *refs):
    parts, out = refs[:4], refs[4]
    for b in range(NB):
        i, j = pos(where[b])
        left, right = rows_of(parts, first, i), tokens_of(hid, j)
        if first:
            left, right = right, left
        out[b] = dot(left, right, TN)


def block_grads(pos, first, where, hid, parts):
    (out,) = call(
        lambda *refs: block_grad_body(pos, first, *refs),
        (where, hid, *parts),
        [((NB, BS, BS), F32)],
        flops=2 * NB * TOK * BS * BS * 4,
        nbytes=4 << 20,
    )
    return out


def sum_body(parts, out):
    total = parts[0].astype(F32)
    for k in range(1, 16):
        total = total + parts[k].astype(F32)
    out[...] = total.astype(BF)


def row_reduce(partial, after):
    parts = lax.all_to_all(partial, ("y", "x"), 0, 0, tiled=True)
    (mine,) = call(
        sum_body,
        (parts,),
        [((32, WT), BF)],
        flops=1 << 20,
        nbytes=2 << 20,
        after=after,
    )
    last = lax.all_to_all(mine, "zh", 0, 0, tiled=True)
    return jnp.sum(last.reshape(4, 8, WT).astype(F32), axis=0).astype(BF)


def shards(inputs, cotangent, w1_blocks, w1_where, w2_blocks, w2_where):
    ids = jnp.stack([lax.axis_index(a) for a in ("core", "zl", "y")]).astype(jnp.int32)
    near = lax.all_gather(jnp.concatenate([inputs, cotangent], axis=0), "zh", axis=0)
    near = near.reshape(4, 2, 8, WT).swapaxes(0, 1).reshape(64, WT)
    along = lax.all_gather(near, "x", axis=0)
    parts = [along] + [shift(along, "y", step) for step in STEPS[1:]]
    weights = (w1_blocks, w2_blocks)
    keep, send = product_terms(ids, w1_where, w2_where, parts[:1], *weights)
    first = column_sums(ids, keep, shift(send, "core", 1))
    keep, send = product_terms(ids, w1_where, w2_where, parts[1:], *weights, after=first[1:])
    second = column_sums(ids, keep, shift(send, "core", 1))
    activated, hidden_grad = call(
        gelu_body, (*first, *second), [((Q, HT), BF)] * 2, flops=1 << 22, nbytes=1 << 20
    )
    whole_hg = lax.all_gather(hidden_grad, ("zl", "core"), axis=0, tiled=True).reshape(8, Q, HT)
    whole_av = lax.all_gather(activated, ("zl", "core"), axis=0, tiled=True).reshape(8, Q, HT)
    partial = input_grad_partial(w1_where, ids, whole_hg, w1_blocks)
    w1_grad = block_grads(w1_pos, 0, w1_where, whole_hg, parts)
    w2_grad = block_grads(w2_pos, 32, w2_where, whole_av, parts)
    input_grad = row_reduce(partial, (whole_av[0, :16, :BS], w1_grad[0, :8]))
    return input_grad, w1_grad, w2_grad


def solution(mesh):
    fine = Mesh(mesh.devices.reshape(4, 4, 4, 4, 2), ("x", "zh", "y", "zl", "core"))
    row, col = ("x", "zh", "y"), ("zl", "core")
    both = row + col
    return jax.shard_map(
        shards,
        mesh=fine,
        in_specs=(P(row, col), P(row, col), P(both, None, None), P(both), P(both, None, None), P(both)),
        out_specs=(P(row, col), P(both, None, None), P(both, None, None)),
        check_vma=False,
    )
```

```python
import math

import jax
import jax.numpy as jnp
from jax import lax
from jax.experimental import pallas as pl
from jax.experimental.pallas import tpu as pltpu
from jax.sharding import Mesh, PartitionSpec as P

BF, F32 = jnp.bfloat16, jnp.float32
BS = 128
TOK = 512
WT = 1536
HT = 768
NI = WT // BS
NJ = HT // BS
NB = 9
Q = TOK // 8
STEPS = (0, 1, 3, 2)
FIRST = Q // 4
W1_COLS = 384
W2_COLS = 96
SIZE = {"x": 4, "y": 4, "zh": 4, "zl": 4, "core": 2}
C0 = math.sqrt(2.0 / math.pi)

VM = pl.BlockSpec(memory_space=pltpu.VMEM)
SM = pl.BlockSpec(memory_space=pltpu.SMEM)


def shift(value, axis, step):
    n = SIZE[axis]
    return lax.ppermute(value, axis, [(i, (i + step) % n) for i in range(n)])


def call(body, ins, outs, scratch=(), flops=0, nbytes=0, vmem=16, after=(), out_space=pltpu.VMEM):
    n, m = len(ins), len(ins) + len(after)
    shape = pltpu.HBM if out_space == pltpu.HBM else jax.ShapeDtypeStruct
    return pl.pallas_call(
        lambda *refs: body(*refs[:n], *refs[m:]),
        out_shape=[shape(s, d) for s, d in outs],
        in_specs=[SM if a.dtype == jnp.int32 else VM for a in ins]
        + [pl.BlockSpec(memory_space=pl.ANY)] * len(after),
        out_specs=[pl.BlockSpec(memory_space=out_space)] * len(outs),
        scratch_shapes=list(scratch),
        compiler_params=pltpu.CompilerParams(vmem_limit_bytes=vmem << 20),
        cost_estimate=pl.CostEstimate(flops=flops, bytes_accessed=nbytes, transcendentals=0),
    )(*ins, *after)


def w1_pos(where):
    return lax.rem(where // W1_COLS, NI), lax.rem(lax.rem(where, W1_COLS), NJ)


def w2_pos(where):
    return lax.rem(lax.rem(where, W2_COLS), NI), lax.rem(where // W2_COLS, NJ)


def lanes(index):
    return pl.ds(pl.multiple_of(index * BS, BS), BS)


NN = (((1,), (0,)), ((), ()))
NT = (((1,), (1,)), ((), ()))
TN = (((0,), (0,)), ((), ()))


def dot(a, b, dims):
    return lax.dot_general(a, b, dims, preferred_element_type=F32)


def rows_of(parts, first, index):
    at = lanes(index + first)
    return jnp.concatenate([p[:, :, at].reshape(4 * 32, BS) for p in parts], axis=0)


def partial_body(where1, where2, ids, *refs):
    parts, (blocks1, blocks2, keep, send, acc) = refs[:-5], refs[-5:]
    n = len(parts) * 16
    core = ids[0]
    acc[...] = jnp.zeros_like(acc)
    for b in range(NB):
        i, j = w1_pos(where1[b])
        acc[j] += dot(rows_of(parts, 0, i), blocks1[b], NN)
        i, j = w2_pos(where2[b])
        acc[NJ + j] += dot(rows_of(parts, NI, i), blocks2[b], NT)
    for z in range(4):
        mine = pl.ds(pl.multiple_of((2 * z + core) * n, n), n)
        other = pl.ds(pl.multiple_of((2 * z + 1 - core) * n, n), n)
        for j in range(2 * NJ):
            keep[z * n : (z + 1) * n, j * BS : (j + 1) * BS] = acc[j, mine]
            send[z * n : (z + 1) * n, j * BS : (j + 1) * BS] = acc[j, other]


def split_body(ids, keep, got, mine, s1, s2, s3):
    n = mine.shape[0]
    zl = ids[1]
    own = pl.ds(pl.multiple_of(zl * n, n), n)
    mine[...] = keep[own] + got[own]
    for k, ref in ((1, s1), (2, s2), (3, s3)):
        part = pl.ds(pl.multiple_of(lax.rem(zl + k, 4) * n, n), n)
        ref[...] = (keep[part] + got[part]).astype(BF)


def product_terms(ids, where1, where2, parts, blocks1, blocks2, after=()):
    n = len(parts)
    return call(
        partial_body,
        (where1, where2, ids, *parts, blocks1, blocks2),
        [((n * Q, WT), F32)] * 2,
        [pltpu.VMEM((2 * NJ, n * 128, BS), F32)],
        flops=2 * NB * n * 128 * BS * BS * 8,
        nbytes=n << 21,
        after=after,
        vmem=20,
    )


def column_sums(ids, keep, got):
    n = keep.shape[0] // 4
    mine, s1, s2, s3 = call(
        split_body,
        (ids, keep, got),
        [((n, WT), F32)] + [((n, WT), BF)] * 3,
        flops=1 << 20,
        nbytes=1 << 20,
    )
    return mine, shift(s1, "zl", 1), shift(s2, "zl", 2), shift(s3, "zl", 3)


def whole_split_body(ids, keep, got, mine, sums):
    n = mine.shape[0]
    own = pl.ds(pl.multiple_of(ids[1] * n, n), n)
    mine[...] = keep[own] + got[own]
    sums[...] = (keep[...] + got[...]).astype(BF)


def column_sums_at_once(ids, keep, got):
    n = keep.shape[0] // 4
    mine, sums = call(
        whole_split_body,
        (ids, keep, got),
        [((n, WT), F32), ((4 * n, WT), BF)],
        flops=1 << 20,
        nbytes=1 << 20,
    )
    return mine, lax.all_to_all(sums, "zl", 0, 0, tiled=True)


def gelu_of(v, g):
    t = jnp.tanh(C0 * (v + 0.044715 * v * v * v))
    derive = C0 * (1.0 + 3.0 * 0.044715 * v * v)
    slope = 0.5 * (1.0 + t) + 0.5 * v * (1.0 - t * t) * derive
    return (0.5 * v * (1.0 + t)).astype(BF), (g * slope).astype(BF)


def gelu_body(ids, own, r1, r2, r3, mine, others, activated, hidden_grad):
    total = own[...] + r1[...].astype(F32) + r2[...].astype(F32) + r3[...].astype(F32)
    activated[:FIRST], hidden_grad[:FIRST] = gelu_of(total[:, :HT], total[:, HT:])
    n = Q - FIRST
    total = mine[...]
    for z in range(4):
        term = others[z * n : (z + 1) * n].astype(F32)
        total = total + jnp.where(ids[1] == z, 0.0, term)
    activated[FIRST:], hidden_grad[FIRST:] = gelu_of(total[:, :HT], total[:, HT:])


def tokens_of(hid, index):
    at = lanes(index)
    return jnp.concatenate(
        [hid[:, :FIRST, at].reshape(8 * FIRST, BS), hid[:, FIRST:, at].reshape(8 * (Q - FIRST), BS)], axis=0
    )


def input_grad_body(where, ids, hg, blocks, out, acc, staged, sems):
    y = ids[2]
    acc[...] = jnp.zeros_like(acc)
    for b in range(NB):
        i, j = w1_pos(where[b])
        acc[i] += dot(tokens_of(hg, j), blocks[b], NT)
    copies = []
    for q, step in enumerate(STEPS):
        for x in range(4):
            row = (4 * q + x) * 32
            for i in range(NI):
                staged[4 * q + x, :, i * BS : (i + 1) * BS] = acc[i, row : row + 32].astype(BF)
        owner = lax.rem(y + 4 - step, 4) * 4
        copies.append(
            pltpu.make_async_copy(staged.at[pl.ds(4 * q, 4)], out.at[pl.ds(owner, 4)], sems.at[q])
        )
        copies[-1].start()
    for copy in copies:
        copy.wait()


def input_grad_partial(where, ids, hg, blocks):
    (out,) = call(
        input_grad_body,
        (where, ids, hg, blocks),
        [((16, 32, WT), BF)],
        [
            pltpu.VMEM((NI, TOK, BS), F32),
            pltpu.VMEM((16, 32, WT), BF),
            pltpu.SemaphoreType.DMA((4,)),
        ],
        out_space=pltpu.HBM,
        flops=2 * NB * TOK * BS * BS * 4,
        nbytes=4 << 20,
    )
    return out


def block_grad_body(pos, first, where, hid, *refs):
    parts, out = refs[:4], refs[4]
    for b in range(NB):
        i, j = pos(where[b])
        left, right = rows_of(parts, first, i), tokens_of(hid, j)
        if first:
            left, right = right, left
        out[b] = dot(left, right, TN)


def block_grads(pos, first, where, hid, parts):
    (out,) = call(
        lambda *refs: block_grad_body(pos, first, *refs),
        (where, hid, *parts),
        [((NB, BS, BS), F32)],
        flops=2 * NB * TOK * BS * BS * 4,
        nbytes=4 << 20,
    )
    return out


def sum_body(parts, out):
    total = parts[0].astype(F32)
    for k in range(1, 16):
        total = total + parts[k].astype(F32)
    out[...] = total.astype(BF)


def row_reduce(partial, after):
    parts = lax.all_to_all(partial, ("y", "x"), 0, 0, tiled=True)
    (mine,) = call(
        sum_body,
        (parts,),
        [((32, WT), BF)],
        flops=1 << 20,
        nbytes=2 << 20,
        after=after,
    )
    last = lax.all_to_all(mine, "zh", 0, 0, tiled=True)
    return jnp.sum(last.reshape(4, 8, WT).astype(F32), axis=0).astype(BF)


def shards(inputs, cotangent, w1_blocks, w1_where, w2_blocks, w2_where):
    ids = jnp.stack([lax.axis_index(a) for a in ("core", "zl", "y")]).astype(jnp.int32)
    both = jnp.concatenate([inputs, cotangent], axis=1)
    near = lax.all_gather(both, "zh", axis=0, tiled=True)
    along = lax.all_gather(near, "x", axis=0)
    parts = [along] + [shift(along, "y", step) for step in STEPS[1:]]
    weights = (w1_blocks, w2_blocks)
    keep, send = product_terms(ids, w1_where, w2_where, parts[:1], *weights)
    first = column_sums(ids, keep, shift(send, "core", 1))
    keep, send = product_terms(ids, w1_where, w2_where, parts[1:], *weights, after=first[1:])
    second = column_sums_at_once(ids, keep, shift(send, "core", 1))
    activated, hidden_grad = call(
        gelu_body, (ids, *first, *second), [((Q, HT), BF)] * 2, flops=1 << 22, nbytes=1 << 20
    )
    whole_hg = lax.all_gather(hidden_grad, ("zl", "core"), axis=0, tiled=True).reshape(8, Q, HT)
    whole_av = lax.all_gather(activated, ("zl", "core"), axis=0, tiled=True).reshape(8, Q, HT)
    partial = input_grad_partial(w1_where, ids, whole_hg, w1_blocks)
    w1_grad = block_grads(w1_pos, 0, w1_where, whole_hg, parts)
    w2_grad = block_grads(w2_pos, NI, w2_where, whole_av, parts)
    input_grad = row_reduce(partial, (whole_av[0, :16, :BS], w1_grad[0, :8]))
    return input_grad, w1_grad, w2_grad


def solution(mesh):
    fine = Mesh(mesh.devices.reshape(4, 4, 4, 4, 2), ("x", "zh", "y", "zl", "core"))
    row, col = ("x", "zh", "y"), ("zl", "core")
    both = row + col
    return jax.shard_map(
        shards,
        mesh=fine,
        in_specs=(P(row, col), P(row, col), P(both, None, None), P(both), P(both, None, None), P(both)),
        out_specs=(P(row, col), P(both, None, None), P(both, None, None)),
        check_vma=False,
    )
```

```python
import math

import jax
import jax.numpy as jnp
from jax import lax
from jax.experimental import pallas as pl
from jax.experimental.pallas import tpu as pltpu
from jax.sharding import Mesh, PartitionSpec as P

BF, F32 = jnp.bfloat16, jnp.float32
BS = 128
TOK = 512
WT = 1536
HT = 768
NI = WT // BS
NJ = HT // BS
NB = 9
Q = TOK // 8
STEPS = (0, 1, 3, 2)
FIRST = Q // 4
W1_COLS = 384
W2_COLS = 96
SIZE = {"x": 4, "y": 4, "zh": 4, "zl": 4, "core": 2}
C0 = math.sqrt(2.0 / math.pi)

VM = pl.BlockSpec(memory_space=pltpu.VMEM)
SM = pl.BlockSpec(memory_space=pltpu.SMEM)


def shift(value, axis, step):
    n = SIZE[axis]
    return lax.ppermute(value, axis, [(i, (i + step) % n) for i in range(n)])


def call(body, ins, outs, scratch=(), flops=0, nbytes=0, vmem=16, after=(), out_space=pltpu.VMEM):
    n, m = len(ins), len(ins) + len(after)
    shape = pltpu.HBM if out_space == pltpu.HBM else jax.ShapeDtypeStruct
    return pl.pallas_call(
        lambda *refs: body(*refs[:n], *refs[m:]),
        out_shape=[shape(s, d) for s, d in outs],
        in_specs=[SM if a.dtype == jnp.int32 else VM for a in ins]
        + [pl.BlockSpec(memory_space=pl.ANY)] * len(after),
        out_specs=[pl.BlockSpec(memory_space=out_space)] * len(outs),
        scratch_shapes=list(scratch),
        compiler_params=pltpu.CompilerParams(vmem_limit_bytes=vmem << 20),
        cost_estimate=pl.CostEstimate(flops=flops, bytes_accessed=nbytes, transcendentals=0),
    )(*ins, *after)


def w1_pos(where):
    return lax.rem(where // W1_COLS, NI), lax.rem(lax.rem(where, W1_COLS), NJ)


def w2_pos(where):
    return lax.rem(lax.rem(where, W2_COLS), NI), lax.rem(where // W2_COLS, NJ)


def lanes(index):
    return pl.ds(pl.multiple_of(index * BS, BS), BS)


NN = (((1,), (0,)), ((), ()))
NT = (((1,), (1,)), ((), ()))
TN = (((0,), (0,)), ((), ()))


def dot(a, b, dims):
    return lax.dot_general(a, b, dims, preferred_element_type=F32)


def rows_of(parts, first, index):
    at = lanes(index + first)
    return jnp.concatenate([p[:, :, at].reshape(4 * 32, BS) for p in parts], axis=0)


def partial_body(where1, where2, ids, *refs):
    parts, (blocks1, blocks2, keep, send, acc) = refs[:-5], refs[-5:]
    n = len(parts) * 16
    core = ids[0]
    acc[...] = jnp.zeros_like(acc)
    for b in range(NB):
        i, j = w1_pos(where1[b])
        acc[j] += dot(rows_of(parts, 0, i), blocks1[b], NN)
        i, j = w2_pos(where2[b])
        acc[NJ + j] += dot(rows_of(parts, NI, i), blocks2[b], NT)
    for z in range(4):
        mine = pl.ds(pl.multiple_of((2 * z + core) * n, n), n)
        other = pl.ds(pl.multiple_of((2 * z + 1 - core) * n, n), n)
        for j in range(2 * NJ):
            keep[z * n : (z + 1) * n, j * BS : (j + 1) * BS] = acc[j, mine]
            send[z * n : (z + 1) * n, j * BS : (j + 1) * BS] = acc[j, other]


def split_body(ids, keep, got, mine, s1, s2, s3):
    n = mine.shape[0]
    zl = ids[1]
    own = pl.ds(pl.multiple_of(zl * n, n), n)
    mine[...] = keep[own] + got[own]
    for k, ref in ((1, s1), (2, s2), (3, s3)):
        part = pl.ds(pl.multiple_of(lax.rem(zl + k, 4) * n, n), n)
        ref[...] = (keep[part] + got[part]).astype(BF)


def product_terms(ids, where1, where2, parts, blocks1, blocks2, after=()):
    n = len(parts)
    return call(
        partial_body,
        (where1, where2, ids, *parts, blocks1, blocks2),
        [((n * Q, WT), F32)] * 2,
        [pltpu.VMEM((2 * NJ, n * 128, BS), F32)],
        flops=2 * NB * n * 128 * BS * BS * 8,
        nbytes=n << 21,
        after=after,
        vmem=20,
    )


def column_sums(ids, keep, got):
    n = keep.shape[0] // 4
    mine, s1, s2, s3 = call(
        split_body,
        (ids, keep, got),
        [((n, WT), F32)] + [((n, WT), BF)] * 3,
        flops=1 << 20,
        nbytes=1 << 20,
    )
    return mine, shift(s1, "zl", 1), shift(s2, "zl", 2), shift(s3, "zl", 3)


def whole_split_body(ids, keep, got, mine, sums):
    n = mine.shape[0]
    own = pl.ds(pl.multiple_of(ids[1] * n, n), n)
    mine[...] = keep[own] + got[own]
    sums[...] = (keep[...] + got[...]).astype(BF)


def column_sums_at_once(ids, keep, got):
    n = keep.shape[0] // 4
    mine, sums = call(
        whole_split_body,
        (ids, keep, got),
        [((n, WT), F32), ((4 * n, WT), BF)],
        flops=1 << 20,
        nbytes=1 << 20,
    )
    return mine, lax.all_to_all(sums, "zl", 0, 0, tiled=True)


def gelu_of(v, g):
    t = jnp.tanh(C0 * (v + 0.044715 * v * v * v))
    derive = C0 * (1.0 + 3.0 * 0.044715 * v * v)
    slope = 0.5 * (1.0 + t) + 0.5 * v * (1.0 - t * t) * derive
    return (0.5 * v * (1.0 + t)).astype(BF), (g * slope).astype(BF)


def gelu_body(ids, own, r1, r2, r3, mine, others, activated, hidden_grad):
    total = own[...] + r1[...].astype(F32) + r2[...].astype(F32) + r3[...].astype(F32)
    activated[:FIRST], hidden_grad[:FIRST] = gelu_of(total[:, :HT], total[:, HT:])
    n = Q - FIRST
    total = mine[...]
    for z in range(4):
        term = others[z * n : (z + 1) * n].astype(F32)
        total = total + jnp.where(ids[1] == z, 0.0, term)
    activated[FIRST:], hidden_grad[FIRST:] = gelu_of(total[:, :HT], total[:, HT:])


def tokens_of(hid, index):
    at = lanes(index)
    return jnp.concatenate(
        [hid[:, :FIRST, at].reshape(8 * FIRST, BS), hid[:, FIRST:, at].reshape(8 * (Q - FIRST), BS)], axis=0
    )


def input_grad_body(where, ids, hg, blocks, out, acc, staged, sems):
    y = ids[2]
    acc[...] = jnp.zeros_like(acc)
    for b in range(NB):
        i, j = w1_pos(where[b])
        acc[i] += dot(tokens_of(hg, j), blocks[b], NT)
    copies = []
    for q, step in enumerate(STEPS):
        for x in range(4):
            row = (4 * q + x) * 32
            for i in range(NI):
                staged[4 * q + x, :, i * BS : (i + 1) * BS] = acc[i, row : row + 32].astype(BF)
        owner = lax.rem(y + 4 - step, 4) * 4
        copies.append(
            pltpu.make_async_copy(staged.at[pl.ds(4 * q, 4)], out.at[pl.ds(owner, 4)], sems.at[q])
        )
        copies[-1].start()
    for copy in copies:
        copy.wait()


def input_grad_partial(where, ids, hg, blocks):
    (out,) = call(
        input_grad_body,
        (where, ids, hg, blocks),
        [((16, 32, WT), BF)],
        [
            pltpu.VMEM((NI, TOK, BS), F32),
            pltpu.VMEM((16, 32, WT), BF),
            pltpu.SemaphoreType.DMA((4,)),
        ],
        out_space=pltpu.HBM,
        flops=2 * NB * TOK * BS * BS * 4,
        nbytes=4 << 20,
    )
    return out


def block_grad_body(pos, first, where, hid, *refs):
    parts, out = refs[:4], refs[4]
    for b in range(NB):
        i, j = pos(where[b])
        left, right = rows_of(parts, first, i), tokens_of(hid, j).astype(BF)
        if first:
            left, right = right, left
        out[b] = dot(left, right, TN)


def block_grads(pos, first, where, hid, parts):
    (out,) = call(
        lambda *refs: block_grad_body(pos, first, *refs),
        (where, hid, *parts),
        [((NB, BS, BS), F32)],
        flops=2 * NB * TOK * BS * BS * 4,
        nbytes=4 << 20,
    )
    return out


def sum_body(parts, out):
    total = parts[0].astype(F32)
    for k in range(1, 16):
        total = total + parts[k].astype(F32)
    out[...] = total.astype(BF)


def last_sum_body(parts, out):
    out[...] = jnp.sum(parts[...].astype(F32).reshape(4, 8, WT), axis=0).astype(BF)


def widen_body(narrow, wide):
    wide[...] = narrow[...].astype(F32)


def row_reduce(partial, after, after_last):
    parts = lax.all_to_all(partial, ("y", "x"), 0, 0, tiled=True)
    (mine,) = call(
        sum_body,
        (parts,),
        [((32, WT), BF)],
        flops=1 << 20,
        nbytes=2 << 20,
        after=after,
    )
    last = lax.all_to_all(mine, "zh", 0, 0, tiled=True)
    (out,) = call(last_sum_body, (last,), [((8, WT), BF)], flops=1 << 16, nbytes=1 << 17, after=after_last)
    return out


def shards(inputs, cotangent, w1_blocks, w1_where, w2_blocks, w2_where):
    ids = jnp.stack([lax.axis_index(a) for a in ("core", "zl", "y")]).astype(jnp.int32)
    both = jnp.concatenate([inputs, cotangent], axis=1)
    near = lax.all_gather(both, "zh", axis=0, tiled=True)
    along = lax.all_gather(near, "x", axis=0)
    parts = [along] + [shift(along, "y", step) for step in STEPS[1:]]
    weights = (w1_blocks, w2_blocks)
    keep, send = product_terms(ids, w1_where, w2_where, parts[:1], *weights)
    first = column_sums(ids, keep, shift(send, "core", 1))
    keep, send = product_terms(ids, w1_where, w2_where, parts[1:], *weights, after=first[1:])
    second = column_sums_at_once(ids, keep, shift(send, "core", 1))
    activated, hidden_grad = call(
        gelu_body, (ids, *first, *second), [((Q, HT), BF)] * 2, flops=1 << 22, nbytes=1 << 20
    )
    whole_hg = lax.all_gather(hidden_grad, ("zl", "core"), axis=0, tiled=True).reshape(8, Q, HT)
    partial = input_grad_partial(w1_where, ids, whole_hg, w1_blocks)
    (wide,) = call(widen_body, (activated,), [((Q, HT), F32)], flops=1 << 16, nbytes=1 << 18, after=(partial,))
    whole_av = lax.all_gather(wide, ("zl", "core"), axis=0)
    w1_grad = block_grads(w1_pos, 0, w1_where, whole_hg, parts)
    w2_grad = block_grads(w2_pos, NI, w2_where, whole_av, parts)
    input_grad = row_reduce(partial, (w1_grad[0, :8],), (w2_grad[0, :8],))
    return input_grad, w1_grad, w2_grad


def solution(mesh):
    fine = Mesh(mesh.devices.reshape(4, 4, 4, 4, 2), ("x", "zh", "y", "zl", "core"))
    row, col = ("x", "zh", "y"), ("zl", "core")
    both = row + col
    return jax.shard_map(
        shards,
        mesh=fine,
        in_specs=(P(row, col), P(row, col), P(both, None, None), P(both), P(both, None, None), P(both)),
        out_specs=(P(row, col), P(both, None, None), P(both, None, None)),
        check_vma=False,
    )
```

```python
import math

import jax
import jax.numpy as jnp
from jax import lax
from jax.experimental import pallas as pl
from jax.experimental.pallas import tpu as pltpu
from jax.sharding import Mesh, PartitionSpec as P

BF, F32 = jnp.bfloat16, jnp.float32
BS = 128
TOK = 512
WT = 1536
HT = 768
NI = WT // BS
NJ = HT // BS
NB = 9
Q = TOK // 8
STEPS = (0, 2, 1, 3)
FIRST = Q // 4
W1_COLS = 384
W2_COLS = 96
SIZE = {"x": 4, "y": 4, "zh": 4, "zl": 4, "core": 2}
C0 = math.sqrt(2.0 / math.pi)

VM = pl.BlockSpec(memory_space=pltpu.VMEM)
SM = pl.BlockSpec(memory_space=pltpu.SMEM)


def shift(value, axis, step):
    n = SIZE[axis]
    return lax.ppermute(value, axis, [(i, (i + step) % n) for i in range(n)])


def call(body, ins, outs, scratch=(), flops=0, nbytes=0, vmem=16, after=(), out_space=pltpu.VMEM):
    n, m = len(ins), len(ins) + len(after)
    shape = pltpu.HBM if out_space == pltpu.HBM else jax.ShapeDtypeStruct
    return pl.pallas_call(
        lambda *refs: body(*refs[:n], *refs[m:]),
        out_shape=[shape(s, d) for s, d in outs],
        in_specs=[SM if a.dtype == jnp.int32 else VM for a in ins]
        + [pl.BlockSpec(memory_space=pl.ANY)] * len(after),
        out_specs=[pl.BlockSpec(memory_space=out_space)] * len(outs),
        scratch_shapes=list(scratch),
        compiler_params=pltpu.CompilerParams(vmem_limit_bytes=vmem << 20),
        cost_estimate=pl.CostEstimate(flops=flops, bytes_accessed=nbytes, transcendentals=0),
    )(*ins, *after)


def w1_pos(where):
    return lax.rem(where // W1_COLS, NI), lax.rem(lax.rem(where, W1_COLS), NJ)


def w2_pos(where):
    return lax.rem(lax.rem(where, W2_COLS), NI), lax.rem(where // W2_COLS, NJ)


def lanes(index):
    return pl.ds(pl.multiple_of(index * BS, BS), BS)


NN = (((1,), (0,)), ((), ()))
NT = (((1,), (1,)), ((), ()))
TN = (((0,), (0,)), ((), ()))


def dot(a, b, dims):
    return lax.dot_general(a, b, dims, preferred_element_type=F32)


def rows_of(parts, first, index):
    at = lanes(index + first)
    return jnp.concatenate([p[:, :, at].reshape(4 * 32, BS) for p in parts], axis=0)


def partial_body(where1, where2, ids, *refs):
    parts, (blocks1, blocks2, keep, send, acc) = refs[:-5], refs[-5:]
    n = len(parts) * 16
    core = ids[0]
    acc[...] = jnp.zeros_like(acc)
    for b in range(NB):
        i, j = w1_pos(where1[b])
        acc[j] += dot(rows_of(parts, 0, i), blocks1[b], NN)
        i, j = w2_pos(where2[b])
        acc[NJ + j] += dot(rows_of(parts, NI, i), blocks2[b], NT)
    for z in range(4):
        mine = pl.ds(pl.multiple_of((2 * z + core) * n, n), n)
        other = pl.ds(pl.multiple_of((2 * z + 1 - core) * n, n), n)
        for j in range(2 * NJ):
            keep[z * n : (z + 1) * n, j * BS : (j + 1) * BS] = acc[j, mine]
            send[z * n : (z + 1) * n, j * BS : (j + 1) * BS] = acc[j, other]


def split_body(ids, keep, got, mine, s1, s2, s3):
    n = mine.shape[0]
    zl = ids[1]
    own = pl.ds(pl.multiple_of(zl * n, n), n)
    mine[...] = keep[own] + got[own]
    for k, ref in ((1, s1), (2, s2), (3, s3)):
        part = pl.ds(pl.multiple_of(lax.rem(zl + k, 4) * n, n), n)
        ref[...] = (keep[part] + got[part]).astype(BF)


def product_terms(ids, where1, where2, parts, blocks1, blocks2, after=()):
    n = len(parts)
    return call(
        partial_body,
        (where1, where2, ids, *parts, blocks1, blocks2),
        [((n * Q, WT), F32)] * 2,
        [pltpu.VMEM((2 * NJ, n * 128, BS), F32)],
        flops=2 * NB * n * 128 * BS * BS * 8,
        nbytes=n << 21,
        after=after,
        vmem=20,
    )


def column_sums(ids, keep, got):
    n = keep.shape[0] // 4
    mine, s1, s2, s3 = call(
        split_body,
        (ids, keep, got),
        [((n, WT), F32)] + [((n, WT), BF)] * 3,
        flops=1 << 20,
        nbytes=1 << 20,
    )
    return mine, shift(s1, "zl", 1), shift(s2, "zl", 2), shift(s3, "zl", 3)


def whole_split_body(ids, keep, got, mine, sums):
    n = mine.shape[0]
    own = pl.ds(pl.multiple_of(ids[1] * n, n), n)
    mine[...] = keep[own] + got[own]
    sums[...] = (keep[...] + got[...]).astype(BF)


def column_sums_at_once(ids, keep, got):
    n = keep.shape[0] // 4
    mine, sums = call(
        whole_split_body,
        (ids, keep, got),
        [((n, WT), F32), ((4 * n, WT), BF)],
        flops=1 << 20,
        nbytes=1 << 20,
    )
    return mine, lax.all_to_all(sums, "zl", 0, 0, tiled=True)


def gelu_of(v, g):
    t = jnp.tanh(C0 * (v + 0.044715 * v * v * v))
    derive = C0 * (1.0 + 3.0 * 0.044715 * v * v)
    slope = 0.5 * (1.0 + t) + 0.5 * v * (1.0 - t * t) * derive
    return (0.5 * v * (1.0 + t)).astype(BF), (g * slope).astype(BF)


def gelu_body(ids, own, r1, r2, r3, mine, others, activated, hidden_grad):
    total = own[...] + r1[...].astype(F32) + r2[...].astype(F32) + r3[...].astype(F32)
    activated[:FIRST], hidden_grad[:FIRST] = gelu_of(total[:, :HT], total[:, HT:])
    n = Q - FIRST
    total = mine[...]
    for z in range(4):
        term = others[z * n : (z + 1) * n].astype(F32)
        total = total + jnp.where(ids[1] == z, 0.0, term)
    activated[FIRST:], hidden_grad[FIRST:] = gelu_of(total[:, :HT], total[:, HT:])


def tokens_of(hid, index):
    at = lanes(index)
    return jnp.concatenate(
        [hid[:, :FIRST, at].reshape(8 * FIRST, BS), hid[:, FIRST:, at].reshape(8 * (Q - FIRST), BS)], axis=0
    )


def input_grad_body(where, ids, hg, blocks, out, acc, staged, sems):
    y = ids[2]
    acc[...] = jnp.zeros_like(acc)
    for b in range(NB):
        i, j = w1_pos(where[b])
        acc[i] += dot(tokens_of(hg, j), blocks[b], NT)
    copies = []
    for q, step in enumerate(STEPS):
        for x in range(4):
            row = (4 * q + x) * 32
            for i in range(NI):
                staged[4 * q + x, :, i * BS : (i + 1) * BS] = acc[i, row : row + 32].astype(BF)
        owner = lax.rem(y + 4 - step, 4) * 4
        copies.append(
            pltpu.make_async_copy(staged.at[pl.ds(4 * q, 4)], out.at[pl.ds(owner, 4)], sems.at[q])
        )
        copies[-1].start()
    for copy in copies:
        copy.wait()


def input_grad_partial(where, ids, hg, blocks):
    (out,) = call(
        input_grad_body,
        (where, ids, hg, blocks),
        [((16, 32, WT), BF)],
        [
            pltpu.VMEM((NI, TOK, BS), F32),
            pltpu.VMEM((16, 32, WT), BF),
            pltpu.SemaphoreType.DMA((4,)),
        ],
        out_space=pltpu.HBM,
        flops=2 * NB * TOK * BS * BS * 4,
        nbytes=4 << 20,
    )
    return out


def block_grad_body(pos, first, where, hid, *refs):
    parts, out = refs[:4], refs[4]
    for b in range(NB):
        i, j = pos(where[b])
        left, right = rows_of(parts, first, i), tokens_of(hid, j)
        if first:
            left, right = right, left
        out[b] = dot(left, right, TN)


def block_grads(pos, first, where, hid, parts):
    (out,) = call(
        lambda *refs: block_grad_body(pos, first, *refs),
        (where, hid, *parts),
        [((NB, BS, BS), F32)],
        flops=2 * NB * TOK * BS * BS * 4,
        nbytes=4 << 20,
    )
    return out


def sum_body(parts, out):
    total = parts[0].astype(F32)
    for k in range(1, 16):
        total = total + parts[k].astype(F32)
    out[...] = total.astype(BF)


def row_reduce(partial, after):
    parts = lax.all_to_all(partial, ("y", "x"), 0, 0, tiled=True)
    (mine,) = call(
        sum_body,
        (parts,),
        [((32, WT), BF)],
        flops=1 << 20,
        nbytes=2 << 20,
        after=after,
    )
    last = lax.all_to_all(mine, "zh", 0, 0, tiled=True)
    return jnp.sum(last.reshape(4, 8, WT).astype(F32), axis=0).astype(BF)


def shards(inputs, cotangent, w1_blocks, w1_where, w2_blocks, w2_where):
    ids = jnp.stack([lax.axis_index(a) for a in ("core", "zl", "y")]).astype(jnp.int32)
    both = jnp.concatenate([inputs, cotangent], axis=1)
    near = lax.all_gather(both, "zh", axis=0, tiled=True)
    along = lax.all_gather(near, "x", axis=0)
    parts = [along] + [shift(along, "y", step) for step in STEPS[1:]]
    weights = (w1_blocks, w2_blocks)
    keep, send = product_terms(ids, w1_where, w2_where, parts[:1], *weights)
    first = column_sums(ids, keep, shift(send, "core", 1))
    keep, send = product_terms(ids, w1_where, w2_where, parts[1:], *weights, after=first[1:])
    second = column_sums_at_once(ids, keep, shift(send, "core", 1))
    activated, hidden_grad = call(
        gelu_body, (ids, *first, *second), [((Q, HT), BF)] * 2, flops=1 << 22, nbytes=1 << 20
    )
    whole_hg = lax.all_gather(hidden_grad, ("zl", "core"), axis=0, tiled=True).reshape(8, Q, HT)
    whole_av = lax.all_gather(activated, ("zl", "core"), axis=0, tiled=True).reshape(8, Q, HT)
    partial = input_grad_partial(w1_where, ids, whole_hg, w1_blocks)
    w1_grad = block_grads(w1_pos, 0, w1_where, whole_hg, parts)
    w2_grad = block_grads(w2_pos, NI, w2_where, whole_av, parts)
    input_grad = row_reduce(partial, (whole_av[0, :16, :BS], w1_grad[0, :8]))
    return input_grad, w1_grad, w2_grad


def solution(mesh):
    fine = Mesh(mesh.devices.reshape(4, 4, 4, 4, 2), ("x", "zh", "y", "zl", "core"))
    row, col = ("x", "zh", "y"), ("zl", "core")
    both = row + col
    return jax.shard_map(
        shards,
        mesh=fine,
        in_specs=(P(row, col), P(row, col), P(both, None, None), P(both), P(both, None, None), P(both)),
        out_specs=(P(row, col), P(both, None, None), P(both, None, None)),
        check_vma=False,
    )
```

```python
import math

import jax
import jax.numpy as jnp
from jax import lax
from jax.experimental import pallas as pl
from jax.experimental.pallas import tpu as pltpu
from jax.sharding import Mesh, PartitionSpec as P

BF, F32 = jnp.bfloat16, jnp.float32
BS = 128
TOK = 512
WT = 1536
HT = 768
NI = WT // BS
NJ = HT // BS
NB = 9
Q = TOK // 8
STEPS = (0, 2, 1, 3)
FIRST = Q // 4
W1_COLS = 384
W2_COLS = 96
SIZE = {"x": 4, "y": 4, "zh": 4, "zl": 4, "core": 2}
C0 = math.sqrt(2.0 / math.pi)

VM = pl.BlockSpec(memory_space=pltpu.VMEM)
SM = pl.BlockSpec(memory_space=pltpu.SMEM)


def shift(value, axis, step):
    n = SIZE[axis]
    return lax.ppermute(value, axis, [(i, (i + step) % n) for i in range(n)])


def call(body, ins, outs, scratch=(), flops=0, nbytes=0, vmem=16, after=(), out_space=pltpu.VMEM):
    n, m = len(ins), len(ins) + len(after)
    shape = pltpu.HBM if out_space == pltpu.HBM else jax.ShapeDtypeStruct
    return pl.pallas_call(
        lambda *refs: body(*refs[:n], *refs[m:]),
        out_shape=[shape(s, d) for s, d in outs],
        in_specs=[SM if a.dtype == jnp.int32 else VM for a in ins]
        + [pl.BlockSpec(memory_space=pl.ANY)] * len(after),
        out_specs=[pl.BlockSpec(memory_space=out_space)] * len(outs),
        scratch_shapes=list(scratch),
        compiler_params=pltpu.CompilerParams(vmem_limit_bytes=vmem << 20),
        cost_estimate=pl.CostEstimate(flops=flops, bytes_accessed=nbytes, transcendentals=0),
    )(*ins, *after)


def w1_pos(where):
    return lax.rem(where // W1_COLS, NI), lax.rem(lax.rem(where, W1_COLS), NJ)


def w2_pos(where):
    return lax.rem(lax.rem(where, W2_COLS), NI), lax.rem(where // W2_COLS, NJ)


def lanes(index):
    return pl.ds(pl.multiple_of(index * BS, BS), BS)


NN = (((1,), (0,)), ((), ()))
NT = (((1,), (1,)), ((), ()))
TN = (((0,), (0,)), ((), ()))


def dot(a, b, dims):
    return lax.dot_general(a, b, dims, preferred_element_type=F32)


def rows_of(parts, first, index):
    at = lanes(index + first)
    return jnp.concatenate([p[:, :, at].reshape(4 * 32, BS) for p in parts], axis=0)


def partial_body(where1, where2, ids, *refs):
    parts, (blocks1, blocks2, keep, send, acc) = refs[:-5], refs[-5:]
    n = len(parts) * 16
    core = ids[0]
    acc[...] = jnp.zeros_like(acc)
    for b in range(NB):
        i, j = w1_pos(where1[b])
        acc[j] += dot(rows_of(parts, 0, i), blocks1[b], NN)
        i, j = w2_pos(where2[b])
        acc[NJ + j] += dot(rows_of(parts, NI, i), blocks2[b], NT)
    for z in range(4):
        mine = pl.ds(pl.multiple_of((2 * z + core) * n, n), n)
        other = pl.ds(pl.multiple_of((2 * z + 1 - core) * n, n), n)
        for j in range(2 * NJ):
            keep[z * n : (z + 1) * n, j * BS : (j + 1) * BS] = acc[j, mine]
            send[z * n : (z + 1) * n, j * BS : (j + 1) * BS] = acc[j, other]


def split_body(ids, keep, got, mine, s1, s2, s3):
    n = mine.shape[0]
    zl = ids[1]
    own = pl.ds(pl.multiple_of(zl * n, n), n)
    mine[...] = keep[own] + got[own]
    for k, ref in ((1, s1), (2, s2), (3, s3)):
        part = pl.ds(pl.multiple_of(lax.rem(zl + k, 4) * n, n), n)
        ref[...] = (keep[part] + got[part]).astype(BF)


def product_terms(ids, where1, where2, parts, blocks1, blocks2, after=()):
    n = len(parts)
    return call(
        partial_body,
        (where1, where2, ids, *parts, blocks1, blocks2),
        [((n * Q, WT), F32)] * 2,
        [pltpu.VMEM((2 * NJ, n * 128, BS), F32)],
        flops=2 * NB * n * 128 * BS * BS * 8,
        nbytes=n << 21,
        after=after,
        vmem=20,
    )


def column_sums(ids, keep, got):
    n = keep.shape[0] // 4
    mine, s1, s2, s3 = call(
        split_body,
        (ids, keep, got),
        [((n, WT), F32)] + [((n, WT), BF)] * 3,
        flops=1 << 20,
        nbytes=1 << 20,
    )
    return mine, shift(s1, "zl", 1), shift(s2, "zl", 2), shift(s3, "zl", 3)


def whole_split_body(ids, keep, got, mine, sums):
    n = mine.shape[0]
    own = pl.ds(pl.multiple_of(ids[1] * n, n), n)
    mine[...] = keep[own] + got[own]
    sums[...] = (keep[...] + got[...]).astype(BF)


def column_sums_at_once(ids, keep, got):
    n = keep.shape[0] // 4
    mine, sums = call(
        whole_split_body,
        (ids, keep, got),
        [((n, WT), F32), ((4 * n, WT), BF)],
        flops=1 << 20,
        nbytes=1 << 20,
    )
    return mine, lax.all_to_all(sums, "zl", 0, 0, tiled=True)


def gelu_of(v, g):
    t = jnp.tanh(C0 * (v + 0.044715 * v * v * v))
    derive = C0 * (1.0 + 3.0 * 0.044715 * v * v)
    slope = 0.5 * (1.0 + t) + 0.5 * v * (1.0 - t * t) * derive
    return (0.5 * v * (1.0 + t)).astype(BF), (g * slope).astype(BF)


def gelu_body(ids, own, r1, r2, r3, mine, others, activated, hidden_grad):
    total = own[...] + r1[...].astype(F32) + r2[...].astype(F32) + r3[...].astype(F32)
    activated[:FIRST], hidden_grad[:FIRST] = gelu_of(total[:, :HT], total[:, HT:])
    n = Q - FIRST
    total = mine[...]
    for z in range(4):
        term = others[z * n : (z + 1) * n].astype(F32)
        total = total + jnp.where(ids[1] == z, 0.0, term)
    activated[FIRST:], hidden_grad[FIRST:] = gelu_of(total[:, :HT], total[:, HT:])


def tokens_of(hid, index):
    at = lanes(index)
    return jnp.concatenate(
        [hid[:, :FIRST, at].reshape(8 * FIRST, BS), hid[:, FIRST:, at].reshape(8 * (Q - FIRST), BS)], axis=0
    )


def input_grad_body(where, ids, hg, blocks, out, acc, staged, sems):
    y = ids[2]
    acc[...] = jnp.zeros_like(acc)
    for b in range(NB):
        i, j = w1_pos(where[b])
        acc[i] += dot(tokens_of(hg, j), blocks[b], NT)
    copies = []
    for q, step in enumerate(STEPS):
        for x in range(4):
            row = (4 * q + x) * 32
            for i in range(NI):
                staged[4 * q + x, :, i * BS : (i + 1) * BS] = acc[i, row : row + 32].astype(BF)
        owner = lax.rem(y + 4 - step, 4) * 4
        copies.append(
            pltpu.make_async_copy(staged.at[pl.ds(4 * q, 4)], out.at[pl.ds(owner, 4)], sems.at[q])
        )
        copies[-1].start()
    for copy in copies:
        copy.wait()


def input_grad_partial(where, ids, hg, blocks):
    (out,) = call(
        input_grad_body,
        (where, ids, hg, blocks),
        [((16, 32, WT), BF)],
        [
            pltpu.VMEM((NI, TOK, BS), F32),
            pltpu.VMEM((16, 32, WT), BF),
            pltpu.SemaphoreType.DMA((4,)),
        ],
        out_space=pltpu.HBM,
        flops=2 * NB * TOK * BS * BS * 4,
        nbytes=4 << 20,
    )
    return out


def block_grad_body(where1, where2, hg, av, *refs):
    parts, (out1, out2) = refs[:4], refs[4:]
    for b in range(NB):
        i, j = w1_pos(where1[b])
        out1[b] = dot(rows_of(parts, 0, i), tokens_of(hg, j), TN)
        i, j = w2_pos(where2[b])
        out2[b] = dot(tokens_of(av, j), rows_of(parts, NI, i), TN)


def block_grads(where1, where2, hg, av, parts):
    return call(
        block_grad_body,
        (where1, where2, hg, av, *parts),
        [((NB, BS, BS), F32)] * 2,
        flops=2 * NB * TOK * BS * BS * 8,
        nbytes=8 << 20,
        vmem=20,
    )


def sum_body(parts, out):
    total = parts[0].astype(F32)
    for k in range(1, 16):
        total = total + parts[k].astype(F32)
    out[...] = total.astype(BF)


def row_reduce(partial, after):
    parts = lax.all_to_all(partial, ("y", "x"), 0, 0, tiled=True)
    (mine,) = call(
        sum_body,
        (parts,),
        [((32, WT), BF)],
        flops=1 << 20,
        nbytes=2 << 20,
        after=after,
    )
    last = lax.all_to_all(mine, "zh", 0, 0, tiled=True)
    return jnp.sum(last.reshape(4, 8, WT).astype(F32), axis=0).astype(BF)


def shards(inputs, cotangent, w1_blocks, w1_where, w2_blocks, w2_where):
    ids = jnp.stack([lax.axis_index(a) for a in ("core", "zl", "y")]).astype(jnp.int32)
    both = jnp.concatenate([inputs, cotangent], axis=1)
    near = lax.all_gather(both, "zh", axis=0, tiled=True)
    along = lax.all_gather(near, "x", axis=0)
    parts = [along] + [shift(along, "y", step) for step in STEPS[1:]]
    weights = (w1_blocks, w2_blocks)
    keep, send = product_terms(ids, w1_where, w2_where, parts[:1], *weights)
    first = column_sums(ids, keep, shift(send, "core", 1))
    keep, send = product_terms(ids, w1_where, w2_where, parts[1:], *weights, after=first[1:])
    second = column_sums_at_once(ids, keep, shift(send, "core", 1))
    activated, hidden_grad = call(
        gelu_body, (ids, *first, *second), [((Q, HT), BF)] * 2, flops=1 << 22, nbytes=1 << 20
    )
    whole_hg = lax.all_gather(hidden_grad, ("zl", "core"), axis=0, tiled=True).reshape(8, Q, HT)
    whole_av = lax.all_gather(activated, ("zl", "core"), axis=0, tiled=True).reshape(8, Q, HT)
    partial = input_grad_partial(w1_where, ids, whole_hg, w1_blocks)
    w1_grad, w2_grad = block_grads(w1_where, w2_where, whole_hg, whole_av, parts)
    input_grad = row_reduce(partial, (w2_grad[0, :8],))
    return input_grad, w1_grad, w2_grad


def solution(mesh):
    fine = Mesh(mesh.devices.reshape(4, 4, 4, 4, 2), ("x", "zh", "y", "zl", "core"))
    row, col = ("x", "zh", "y"), ("zl", "core")
    both = row + col
    return jax.shard_map(
        shards,
        mesh=fine,
        in_specs=(P(row, col), P(row, col), P(both, None, None), P(both), P(both, None, None), P(both)),
        out_specs=(P(row, col), P(both, None, None), P(both, None, None)),
        check_vma=False,
    )
```

```python
import math

import jax
import jax.numpy as jnp
from jax import lax
from jax.experimental import pallas as pl
from jax.experimental.pallas import tpu as pltpu
from jax.sharding import Mesh, PartitionSpec as P

BF, F32 = jnp.bfloat16, jnp.float32
BS = 128
TOK = 512
WT = 1536
HT = 768
NI = WT // BS
NJ = HT // BS
NB = 9
Q = TOK // 8
STEPS = (0, 3, 1, 2)
FIRST = Q // 4
W1_COLS = 384
W2_COLS = 96
SIZE = {"x": 4, "y": 4, "zh": 4, "zl": 4, "core": 2}
C0 = math.sqrt(2.0 / math.pi)

VM = pl.BlockSpec(memory_space=pltpu.VMEM)
SM = pl.BlockSpec(memory_space=pltpu.SMEM)


def shift(value, axis, step):
    n = SIZE[axis]
    return lax.ppermute(value, axis, [(i, (i + step) % n) for i in range(n)])


def call(body, ins, outs, scratch=(), flops=0, nbytes=0, vmem=16, after=(), out_space=pltpu.VMEM):
    n, m = len(ins), len(ins) + len(after)
    shape = pltpu.HBM if out_space == pltpu.HBM else jax.ShapeDtypeStruct
    return pl.pallas_call(
        lambda *refs: body(*refs[:n], *refs[m:]),
        out_shape=[shape(s, d) for s, d in outs],
        in_specs=[SM if a.dtype == jnp.int32 else VM for a in ins]
        + [pl.BlockSpec(memory_space=pl.ANY)] * len(after),
        out_specs=[pl.BlockSpec(memory_space=out_space)] * len(outs),
        scratch_shapes=list(scratch),
        compiler_params=pltpu.CompilerParams(vmem_limit_bytes=vmem << 20),
        cost_estimate=pl.CostEstimate(flops=flops, bytes_accessed=nbytes, transcendentals=0),
    )(*ins, *after)


def w1_pos(where):
    return lax.rem(where // W1_COLS, NI), lax.rem(lax.rem(where, W1_COLS), NJ)


def w2_pos(where):
    return lax.rem(lax.rem(where, W2_COLS), NI), lax.rem(where // W2_COLS, NJ)


def lanes(index):
    return pl.ds(pl.multiple_of(index * BS, BS), BS)


NN = (((1,), (0,)), ((), ()))
NT = (((1,), (1,)), ((), ()))
TN = (((0,), (0,)), ((), ()))


def dot(a, b, dims):
    return lax.dot_general(a, b, dims, preferred_element_type=F32)


def rows_of(parts, first, index):
    at = lanes(index + first)
    return jnp.concatenate([p[:, :, at].reshape(4 * 32, BS) for p in parts], axis=0)


def partial_body(where1, where2, ids, *refs):
    parts, (blocks1, blocks2, keep, send, acc) = refs[:-5], refs[-5:]
    n = len(parts) * 16
    core = ids[0]
    acc[...] = jnp.zeros_like(acc)
    for b in range(NB):
        i, j = w1_pos(where1[b])
        acc[j] += dot(rows_of(parts, 0, i), blocks1[b], NN)
        i, j = w2_pos(where2[b])
        acc[NJ + j] += dot(rows_of(parts, NI, i), blocks2[b], NT)
    for z in range(4):
        mine = pl.ds(pl.multiple_of((2 * z + core) * n, n), n)
        other = pl.ds(pl.multiple_of((2 * z + 1 - core) * n, n), n)
        for j in range(2 * NJ):
            keep[z * n : (z + 1) * n, j * BS : (j + 1) * BS] = acc[j, mine]
            send[z * n : (z + 1) * n, j * BS : (j + 1) * BS] = acc[j, other]


def split_body(ids, keep, got, mine, s1, s2, s3):
    n = mine.shape[0]
    zl = ids[1]
    own = pl.ds(pl.multiple_of(zl * n, n), n)
    mine[...] = keep[own] + got[own]
    for k, ref in ((1, s1), (2, s2), (3, s3)):
        part = pl.ds(pl.multiple_of(lax.rem(zl + k, 4) * n, n), n)
        ref[...] = (keep[part] + got[part]).astype(BF)


def product_terms(ids, where1, where2, parts, blocks1, blocks2, after=()):
    n = len(parts)
    return call(
        partial_body,
        (where1, where2, ids, *parts, blocks1, blocks2),
        [((n * Q, WT), F32)] * 2,
        [pltpu.VMEM((2 * NJ, n * 128, BS), F32)],
        flops=2 * NB * n * 128 * BS * BS * 8,
        nbytes=n << 21,
        after=after,
        vmem=20,
    )


def column_sums(ids, keep, got):
    n = keep.shape[0] // 4
    mine, s1, s2, s3 = call(
        split_body,
        (ids, keep, got),
        [((n, WT), F32)] + [((n, WT), BF)] * 3,
        flops=1 << 20,
        nbytes=1 << 20,
    )
    return mine, shift(s1, "zl", 1), shift(s2, "zl", 2), shift(s3, "zl", 3)


def whole_split_body(ids, keep, got, mine, sums):
    n = mine.shape[0]
    own = pl.ds(pl.multiple_of(ids[1] * n, n), n)
    mine[...] = keep[own] + got[own]
    sums[...] = (keep[...] + got[...]).astype(BF)


def column_sums_at_once(ids, keep, got):
    n = keep.shape[0] // 4
    mine, sums = call(
        whole_split_body,
        (ids, keep, got),
        [((n, WT), F32), ((4 * n, WT), BF)],
        flops=1 << 20,
        nbytes=1 << 20,
    )
    return mine, lax.all_to_all(sums, "zl", 0, 0, tiled=True)


def gelu_of(v, g):
    t = jnp.tanh(C0 * (v + 0.044715 * v * v * v))
    derive = C0 * (1.0 + 3.0 * 0.044715 * v * v)
    slope = 0.5 * (1.0 + t) + 0.5 * v * (1.0 - t * t) * derive
    return (0.5 * v * (1.0 + t)).astype(BF), (g * slope).astype(BF)


def gelu_body(ids, own, r1, r2, r3, mine, others, activated, hidden_grad):
    total = own[...] + r1[...].astype(F32) + r2[...].astype(F32) + r3[...].astype(F32)
    activated[:FIRST], hidden_grad[:FIRST] = gelu_of(total[:, :HT], total[:, HT:])
    n = Q - FIRST
    total = mine[...]
    for z in range(4):
        term = others[z * n : (z + 1) * n].astype(F32)
        total = total + jnp.where(ids[1] == z, 0.0, term)
    activated[FIRST:], hidden_grad[FIRST:] = gelu_of(total[:, :HT], total[:, HT:])


def tokens_of(hid, index):
    at = lanes(index)
    return jnp.concatenate(
        [hid[:, :FIRST, at].reshape(8 * FIRST, BS), hid[:, FIRST:, at].reshape(8 * (Q - FIRST), BS)], axis=0
    )


def input_grad_body(where, ids, hg, blocks, out, acc, staged, sems):
    y = ids[2]
    acc[...] = jnp.zeros_like(acc)
    for b in range(NB):
        i, j = w1_pos(where[b])
        acc[i] += dot(tokens_of(hg, j), blocks[b], NT)
    copies = []
    for q, step in enumerate(STEPS):
        for x in range(4):
            row = (4 * q + x) * 32
            for i in range(NI):
                staged[4 * q + x, :, i * BS : (i + 1) * BS] = acc[i, row : row + 32].astype(BF)
        owner = lax.rem(y + 4 - step, 4) * 4
        copies.append(
            pltpu.make_async_copy(staged.at[pl.ds(4 * q, 4)], out.at[pl.ds(owner, 4)], sems.at[q])
        )
        copies[-1].start()
    for copy in copies:
        copy.wait()


def input_grad_partial(where, ids, hg, blocks):
    (out,) = call(
        input_grad_body,
        (where, ids, hg, blocks),
        [((16, 32, WT), BF)],
        [
            pltpu.VMEM((NI, TOK, BS), F32),
            pltpu.VMEM((16, 32, WT), BF),
            pltpu.SemaphoreType.DMA((4,)),
        ],
        out_space=pltpu.HBM,
        flops=2 * NB * TOK * BS * BS * 4,
        nbytes=4 << 20,
    )
    return out


def block_grad_body(where1, where2, hg, av, *refs):
    parts, (out1, out2) = refs[:4], refs[4:]
    for b in range(NB):
        i, j = w1_pos(where1[b])
        out1[b] = dot(rows_of(parts, 0, i), tokens_of(hg, j), TN)
        i, j = w2_pos(where2[b])
        out2[b] = dot(tokens_of(av, j), rows_of(parts, NI, i), TN)


def block_grads(where1, where2, hg, av, parts):
    return call(
        block_grad_body,
        (where1, where2, hg, av, *parts),
        [((NB, BS, BS), F32)] * 2,
        flops=2 * NB * TOK * BS * BS * 8,
        nbytes=8 << 20,
        vmem=20,
    )


def sum_body(parts, out):
    total = parts[0].astype(F32)
    for k in range(1, 16):
        total = total + parts[k].astype(F32)
    out[...] = total.astype(BF)


def row_reduce(partial, after):
    parts = lax.all_to_all(partial, ("y", "x"), 0, 0, tiled=True)
    (mine,) = call(
        sum_body,
        (parts,),
        [((32, WT), BF)],
        flops=1 << 20,
        nbytes=2 << 20,
        after=after,
    )
    last = lax.all_to_all(mine, "zh", 0, 0, tiled=True)
    return jnp.sum(last.reshape(4, 8, WT).astype(F32), axis=0).astype(BF)


def shards(inputs, cotangent, w1_blocks, w1_where, w2_blocks, w2_where):
    ids = jnp.stack([lax.axis_index(a) for a in ("core", "zl", "y")]).astype(jnp.int32)
    both = jnp.concatenate([inputs, cotangent], axis=1)
    near = lax.all_gather(both, "zh", axis=0, tiled=True)
    along = lax.all_gather(near, "x", axis=0)
    parts = [along] + [shift(along, "y", step) for step in STEPS[1:]]
    weights = (w1_blocks, w2_blocks)
    keep, send = product_terms(ids, w1_where, w2_where, parts[:1], *weights)
    first = column_sums(ids, keep, shift(send, "core", 1))
    keep, send = product_terms(ids, w1_where, w2_where, parts[1:], *weights, after=first[1:])
    second = column_sums_at_once(ids, keep, shift(send, "core", 1))
    activated, hidden_grad = call(
        gelu_body, (ids, *first, *second), [((Q, HT), BF)] * 2, flops=1 << 22, nbytes=1 << 20
    )
    whole_hg = lax.all_gather(hidden_grad, ("zl", "core"), axis=0, tiled=True).reshape(8, Q, HT)
    whole_av = lax.all_gather(activated, ("zl", "core"), axis=0, tiled=True).reshape(8, Q, HT)
    partial = input_grad_partial(w1_where, ids, whole_hg, w1_blocks)
    w1_grad, w2_grad = block_grads(w1_where, w2_where, whole_hg, whole_av, parts)
    input_grad = row_reduce(partial, (w2_grad[0, :8],))
    return input_grad, w1_grad, w2_grad


def solution(mesh):
    fine = Mesh(mesh.devices.reshape(4, 4, 4, 4, 2), ("x", "zh", "y", "zl", "core"))
    row, col = ("x", "zh", "y"), ("zl", "core")
    both = row + col
    return jax.shard_map(
        shards,
        mesh=fine,
        in_specs=(P(row, col), P(row, col), P(both, None, None), P(both), P(both, None, None), P(both)),
        out_specs=(P(row, col), P(both, None, None), P(both, None, None)),
        check_vma=False,
    )
```
